32 devices in a mesh: replica: 2 (over x), fsdp: 16 (over z, y, core).
Axes of the slice: x: 2, y: 2, z: 4, core: 2. Of those that a mesh axis runs over, the one named last changes fastest.
Arguments:
- tokens_in: bfloat16 [4, 32, 197, 384], P(None, ('replica', 'fsdp')), may hold values from -6 to 6
- picks_in: int32 [4, 32, 197, 2], P(None, ('replica', 'fsdp')), may hold values from 0 to 31, all different within a row
- ranks_in: int32 [4, 32, 197], P(None, ('replica', 'fsdp')), may hold values from 0 to 196, each once within a row
- capacity: int32 [32], replicated, may hold values from 9 to 16, as said below
- first_gain: bfloat16 [384], P('fsdp'), may hold values from 0.5 to 1.5
- first_shift: bfloat16 [384], P('fsdp'), may hold values from -1 to 1
- attend_weight: bfloat16 [384, 1152], P('fsdp'), may hold values from -0.3125 to 0.3125
- output_weight: bfloat16 [384, 384], P('fsdp'), may hold values from -1.21875 to 1.21875
- second_gain: bfloat16 [384], P('fsdp'), may hold values from 0.5 to 1.5
- second_shift: bfloat16 [384], P('fsdp'), may hold values from -1 to 1
- router_weight: bfloat16 [384, 32], P('fsdp'), may hold values from -0.21386719 to 0.21386719
- expert_up: bfloat16 [32, 384, 1536], P('fsdp'), may hold values from -0.3125 to 0.3125
- expert_down: bfloat16 [32, 1536, 384], P('fsdp'), may hold values from -3.671875 to 3.671875
- cotangent: bfloat16 [4, 32, 197, 384], P(None, ('replica', 'fsdp')), may hold values from -6 to 6
Outputs:
- block_out: bfloat16 [4, 32, 197, 384], P(None, ('replica', 'fsdp'))
- input_gradient: bfloat16 [4, 32, 197, 384], P(None, ('replica', 'fsdp'))
- first_gain_gradient: float32 [384], P('fsdp')
- first_shift_gradient: float32 [384], P('fsdp')
- attend_gradient: float32 [384, 1152], P('fsdp')
- output_gradient: float32 [384, 384], P('fsdp')
- second_gain_gradient: float32 [384], P('fsdp')
- second_shift_gradient: float32 [384], P('fsdp')
- router_gradient: float32 [384, 32], P('fsdp')
- expert_up_gradient: float32 [32, 384, 1536], P('fsdp')
- expert_down_gradient: float32 [32, 1536, 384], P('fsdp')
The draws below stay inside these ranges and needn't reach their ends.
Inputs may be any that keep to these rules, and one draw needn't show every extreme that they name: `picks_in`: each row names two different experts. `ranks_in`: within an image the ranks are the numbers 0 to 196, each once. `capacity`: some expert has exactly 16.
All inputs are finite; a program needn't handle non-finite values.
Results may differ from the reference program's by a relative error of at most 0.022.
Values may be sent and summed in bfloat16 or wider, within the bound.
No kernel may reach another device: no remote copies, remote signals or barrier semaphores. Data moves between devices by JAX's collectives and lax.ppermute only.
A program may use at most 128 MiB of HBM per device.

```python
import jax
import jax.numpy as jnp
from jax import lax

D = 384
HEADS = 6
HEAD_DIM = 64
FF = 1536
SEQ = 197
CAP = 16
MB = 4
EXP = 32
IMAGES = 32


def draw_capacity(key, part):
    key = jax.random.fold_in(key, 11)
    first_key, second_key = jax.random.split(key)
    base = jax.random.randint(first_key, (EXP,), CAP // 2 + 1, CAP + 1, dtype=jnp.int32)
    chosen = jax.random.randint(second_key, (), 0, EXP, dtype=jnp.int32)
    labels = jnp.arange(EXP, dtype=jnp.int32)
    return jnp.where(labels == chosen, CAP, base).astype(jnp.int32)


def level_of(rng, shape, shards, smallest, largest):
    def one(axis_at, blocks):
        draws = jax.random.uniform(jax.random.fold_in(jax.random.fold_in(rng, 6), axis_at), (blocks,), jnp.float32, smallest / len(shards), largest / len(shards))
        return jnp.repeat(jnp.exp(draws), shape[axis_at] // blocks).reshape((-1,) + (1,) * (len(shape) - axis_at - 1))

    loudness = one(*shards[0])
    for cut in shards[1:]:
        loudness = loudness * one(*cut)
    return loudness


def different_ones(stream_key, rows, number_of, top, lift):
    order = jax.random.permutation(jax.random.fold_in(stream_key, 1), number_of)
    favour = order
    for power in range(3):
        favour = favour * favour // number_of
    favour = favour * lift // number_of
    lots = jax.random.randint(jax.random.fold_in(stream_key, 2), (rows, number_of), 0, 4096) + favour
    sure = jax.random.permutation(jax.random.fold_in(stream_key, 3), rows)[jnp.arange(number_of) % rows]
    lots = jnp.where(jnp.arange(rows)[:, None] == sure[None, :], 1 << 14, lots)
    score = lots * number_of + jnp.arange(number_of)
    return lax.top_k(score.astype(jnp.int32), top)[1].astype(jnp.int32)


def centred(key, shape, deviation, most, shards=(), kind=jnp.bfloat16):
    array = jax.random.normal(key, shape, jnp.float32) * deviation
    if len(shards) > 0:
        array = level_of(key, shape, shards, -0.22, 0.18) * array
    return jnp.clip(array, min=-most, max=most).astype(kind)


def setup_inputs(seed: int = 0) -> dict:
    seeds = jax.random.split(jax.random.key(seed), 15)
    tokens_in = centred(seeds[0], (MB, IMAGES, SEQ, D), 1.0, 6.0, ((1, 32),))
    picks_in = different_ones(seeds[1], MB * IMAGES * SEQ, EXP, 2, 512).reshape((MB, IMAGES, SEQ, 2))
    ranks_in = jax.vmap(lambda own: jax.random.permutation(own, SEQ))(jax.random.split(seeds[2], MB * IMAGES)).reshape((MB, IMAGES, SEQ)).astype(jnp.int32)
    capacity = draw_capacity(jax.random.fold_in(seeds[14], 71), 0)
    first_gain = jnp.clip(1.0 + 0.1 * jax.random.normal(seeds[4], (D,), jnp.float32), 0.5, 1.5).astype(jnp.bfloat16)
    first_shift = centred(seeds[5], (D,), 0.2, 1.0, ((0, 16),))
    attend_weight = centred(seeds[6], (D, 3 * D), D ** -0.5, 0.3125, ((0, 16),))
    output_weight = centred(seeds[7], (D, D), (4.0 * D ** -0.5), 1.21875, ((0, 16),))
    second_gain = jnp.clip(1.0 + 0.1 * jax.random.normal(seeds[8], (D,), jnp.float32), 0.5, 1.5).astype(jnp.bfloat16)
    second_shift = centred(seeds[9], (D,), 0.2, 1.0, ((0, 16),))
    router_weight = centred(seeds[10], (D, EXP), (0.7 * D ** -0.5), 0.21386719, ((0, 16),))
    expert_up = centred(seeds[11], (EXP, D, FF), D ** -0.5, 0.3125, ((0, 16),))
    expert_down = centred(seeds[12], (EXP, FF, D), (0.75 * EXP * FF ** -0.5), 3.671875, ((0, 16),))
    cotangent = centred(seeds[13], (MB, IMAGES, SEQ, D), 1.0, 6.0, ((1, 32),))
    return dict(tokens_in=tokens_in, picks_in=picks_in, ranks_in=ranks_in, capacity=capacity, first_gain=first_gain, first_shift=first_shift, attend_weight=attend_weight, output_weight=output_weight, second_gain=second_gain, second_shift=second_shift, router_weight=router_weight, expert_up=expert_up, expert_down=expert_down, cotangent=cotangent)


EPSILON = 1e-06
HIGH = lax.Precision.HIGHEST

@jax.custom_vjp
def low(v):
    return lax.optimization_barrier(v.astype(jnp.bfloat16)).astype(jnp.float32)

@jax.custom_vjp
def low_back(v):
    return v

def low_keep(v):
    return (low(v), None)

def low_pass(kept, grad):
    return (grad,)

def back_keep(v):
    return (v, None)

def back_low(kept, grad):
    return (low(grad),)
low.defvjp(low_keep, low_pass)
low_back.defvjp(back_keep, back_low)

def both_round(value):
    return low_back(low(value))

def layer_norm(values, gain, shift):
    center = values - lax.optimization_barrier(jnp.mean(values, axis=-1, keepdims=True))
    spread = lax.optimization_barrier(jnp.mean(center * center, axis=-1, keepdims=True))
    return center * lax.rsqrt(spread + EPSILON) * gain + shift

def route(picks, ranks, capacity):
    length = picks.shape[0]
    experts = jnp.concatenate([picks[:, 0], picks[:, 1]]).astype(jnp.int32)
    order = jnp.concatenate([ranks, ranks + length]).astype(jnp.int32)
    same = experts[:, None] == experts[None, :]
    earlier = order[None, :] < order[:, None]
    position = lax.optimization_barrier(jnp.sum((same & earlier).astype(jnp.int32), axis=1))
    labels = jnp.arange(capacity.shape[0], dtype=jnp.int32)
    limit = lax.optimization_barrier(jnp.sum(jnp.where(experts[:, None] == labels[None, :], capacity[None, :], 0), axis=1))
    kept = position < limit
    slot = jnp.where(kept, experts * CAP + position, 0).astype(jnp.int32)
    return (slot.reshape(2, length).T, kept.reshape(2, length).T)

def forward(params, tokens, picks, ranks, capacity):
    first_gain, first_shift, attend, output, second_gain, second_shift, router, expert_up, expert_down = params
    length = tokens.shape[0]
    normed = low(layer_norm(tokens, first_gain, first_shift))
    joined = jnp.dot(normed, attend, precision=HIGH)
    queries = both_round(joined[:, :D]).reshape(length, HEADS, HEAD_DIM)
    keys = both_round(joined[:, D:2 * D]).reshape(length, HEADS, HEAD_DIM)
    values = both_round(joined[:, 2 * D:]).reshape(length, HEADS, HEAD_DIM)
    scores = low_back(jnp.einsum('qhd,khd->hqk', queries, keys, precision=HIGH) * HEAD_DIM ** (-0.5))
    probs = jax.nn.softmax(scores, axis=-1)
    mixed = jnp.einsum('hqk,khd->qhd', low(probs), values, precision=HIGH).reshape(length, D)
    mixed = both_round(mixed)
    branch = low_back(jnp.dot(mixed, output, precision=HIGH))
    middle = tokens + branch
    second = low(layer_norm(middle, second_gain, second_shift))
    logits = low_back(jnp.dot(second, router, precision=HIGH))
    gates = jax.nn.softmax(logits, axis=-1)
    slot, kept = route(picks, ranks, capacity)
    rows = jnp.arange(EXP * CAP, dtype=jnp.int32)
    table = jnp.zeros((EXP * CAP, length), jnp.float32)
    for choice_index in range(2):
        hit = (rows[:, None] == slot[None, :, choice_index]) & kept[None, :, choice_index]
        table = table + jnp.where(hit, jnp.float32(1.0), jnp.float32(0.0))
    dispatched = low_back(jnp.dot(table, second, precision=HIGH)).reshape(EXP, CAP, D)
    pre = low_back(jnp.einsum('ecd,edf->ecf', dispatched, expert_up, precision=HIGH))
    hidden = low(jax.nn.gelu(pre, approximate=False))
    returned = both_round(jnp.einsum('ecf,efd->ecd', hidden, expert_down, precision=HIGH)).reshape(EXP * CAP, D)
    chosen = jnp.take_along_axis(gates, picks, axis=1)
    result = middle
    for choice_index in range(2):
        weight = jnp.where(kept[:, choice_index], chosen[:, choice_index], jnp.float32(0.0))
        result = result + weight[:, None] * jnp.take(returned, slot[:, choice_index], axis=0)
    return result

def reference(tokens_in, picks_in, ranks_in, capacity, first_gain, first_shift, attend_weight, output_weight, second_gain, second_shift, router_weight, expert_up, expert_down, cotangent):
    params = tuple((weight.astype(jnp.float32) for weight in (first_gain, first_shift, attend_weight, output_weight, second_gain, second_shift, router_weight, expert_up, expert_down)))
    flat_tokens = tokens_in.reshape(-1, SEQ, D).astype(jnp.float32)
    flat_picks = picks_in.reshape(-1, SEQ, 2).astype(jnp.int32)
    flat_ranks = ranks_in.reshape(-1, SEQ).astype(jnp.int32)
    flat_cot = cotangent.reshape(-1, SEQ, D).astype(jnp.float32)

    def step(total, item):
        tokens, picks, ranks, incoming = item
        result, pull = jax.vjp(lambda weights, inputs: forward(weights, inputs, picks, ranks, capacity), params, tokens)
        grad_params, grad_tokens = pull(incoming)
        total = jax.tree.map(lambda left, right: left + right, total, grad_params)
        return (total, (result.astype(jnp.bfloat16), grad_tokens.astype(jnp.bfloat16)))
    zeros = jax.tree.map(jnp.zeros_like, params)
    total, outputs = lax.scan(step, zeros, (flat_tokens, flat_picks, flat_ranks, flat_cot))
    results = outputs[0].reshape(tokens_in.shape)
    gradients = outputs[1].reshape(tokens_in.shape)
    return (results, gradients, total[0], total[1], total[2], total[3], total[4], total[5], total[6], total[7], total[8])
```

```python
import jax
import jax.numpy as jnp
from jax import lax
from jax.sharding import PartitionSpec as P

HEADS = 6
HEAD_DIM = 64
CAP = 16
EPSILON = 1e-06
BF = jnp.bfloat16
F32 = jnp.float32


def dot(a, b, ca, cb):
    return lax.dot_general(a, b, (((ca,), (cb,)), ((), ())), preferred_element_type=F32)


def layer_norm(values, gain, shift):
    center = values - jnp.mean(values, axis=-1, keepdims=True)
    spread = jnp.mean(center * center, axis=-1, keepdims=True)
    return center * lax.rsqrt(spread + EPSILON) * gain + shift


def norm_parts(values):
    center = values - jnp.mean(values, axis=-1, keepdims=True)
    inv = lax.rsqrt(jnp.mean(center * center, axis=-1, keepdims=True) + EPSILON)
    return center * inv, inv


def norm_back(grad, hat, inv, gain):
    scaled = grad * gain
    return inv * (
        scaled
        - jnp.mean(scaled, axis=-1, keepdims=True)
        - hat * jnp.mean(scaled * hat, axis=-1, keepdims=True)
    )


def route(picks, ranks, capacity):
    labels = jnp.arange(capacity.shape[0], dtype=jnp.int32)
    earlier = (ranks[None, :] < ranks[:, None]).astype(BF)
    hits = [(picks[:, c, None] == labels[None, :]) for c in range(2)]
    ones = [h.astype(BF) for h in hits]
    before = [dot(earlier, ones[0], 1, 0)]
    before.append(dot(earlier, ones[1], 1, 0) + jnp.sum(ones[0].astype(F32), 0, keepdims=True))
    slots = []
    for c in range(2):
        position = jnp.sum(jnp.where(hits[c], before[c], 0.0), axis=1).astype(jnp.int32)
        limit = jnp.sum(jnp.where(hits[c], capacity[None, :], 0), axis=1)
        slots.append(jnp.where(position < limit, picks[:, c] * CAP + position, -1))
    return slots


def solution(mesh):
    replicas = mesh.shape["replica"]

    def body(tokens_in, picks_in, ranks_in, capacity, first_gain, first_shift, attend_weight,
             output_weight, second_gain, second_shift, router_weight, expert_up, expert_down, cotangent):
        micro, _, length, width = tokens_in.shape
        experts = capacity.shape[0]
        groups = lax.axis_size("fsdp")
        local = expert_up.shape[0]
        slots = experts * CAP
        scale = HEAD_DIM ** (-0.5)
        packed = jnp.concatenate(
            [attend_weight, output_weight, router_weight]
            + [v[:, None] for v in (first_gain, first_shift, second_gain, second_shift)], axis=1)
        cols = packed.shape[1]
        packed = jnp.pad(packed, ((0, 0), (0, -cols % 128)))
        full = lax.all_gather(packed, "fsdp", axis=0, tiled=True)
        attend = full[:, : 3 * width]
        output = full[:, 3 * width : 4 * width]
        router = full[:, 4 * width : 4 * width + experts]
        vecs = full[:, 4 * width + experts : cols].astype(F32).T
        gain_one, shift_one, gain_two, shift_two = (vecs[i][None] for i in range(4))

        tokens = tokens_in[:, 0].astype(F32)
        incoming = cotangent[:, 0].astype(F32)
        slot_ids = jax.vmap(lambda p, r: route(p, r, capacity))(picks_in[:, 0], ranks_in[:, 0])
        rows = jnp.arange(slots, dtype=jnp.int32)
        table = ((slot_ids[0][:, None, :] == rows[None, :, None])
                 | (slot_ids[1][:, None, :] == rows[None, :, None])).astype(BF)

        def exchange(rows_):
            r = rows_.reshape(micro, groups, local * CAP, width).transpose(1, 0, 2, 3)
            return lax.all_to_all(r, "fsdp", split_axis=0, concat_axis=0, tiled=True)

        def come_back(r):
            r = lax.all_to_all(r, "fsdp", split_axis=0, concat_axis=0, tiled=True)
            return r.transpose(1, 0, 2, 3).reshape(micro, slots, width)

        def pick_rows(v):
            return jnp.einsum("mst,mtd->msd", table, v, preferred_element_type=F32).astype(BF)

        def to_expert(r):
            return r.reshape(groups, micro, local, CAP, width).transpose(2, 0, 1, 3, 4).reshape(local, -1, width)

        def from_expert(r):
            return r.reshape(local, groups, micro, CAP, width).transpose(1, 2, 0, 3, 4).reshape(
                groups, micro, local * CAP, width)

        def swap(v):
            return lax.ppermute(v, "replica", [(0, 1), (1, 0)])

        cot_rows = exchange(pick_rows(cotangent[:, 0]))

        hat_one, inv_one = norm_parts(tokens)
        normed = (hat_one * gain_one + shift_one).astype(BF)
        joined = jnp.einsum("mtd,de->mte", normed, attend, preferred_element_type=F32).astype(BF)
        heads = joined.reshape(micro, length, 3, HEADS, HEAD_DIM)
        queries, keys, values = heads[:, :, 0], heads[:, :, 1], heads[:, :, 2]
        scores = jnp.einsum("mqhd,mkhd->mhqk", queries, keys, preferred_element_type=F32) * scale
        raised = jnp.exp(scores - jnp.max(scores, axis=-1, keepdims=True))
        probs = raised / jnp.sum(raised, axis=-1, keepdims=True)
        probs_low = probs.astype(BF)
        mixed = jnp.einsum("mhqk,mkhd->mqhd", probs_low, values, preferred_element_type=F32)
        mixed = mixed.reshape(micro, length, width).astype(BF)
        middle = tokens + jnp.einsum("mtd,de->mte", mixed, output, preferred_element_type=F32)
        hat_two, inv_two = norm_parts(middle)
        second = (hat_two * gain_two + shift_two).astype(BF)
        rows_in = exchange(pick_rows(second))

        x = to_expert(rows_in)
        gx = to_expert(cot_rows)
        first_label = lax.axis_index("fsdp") * local
        own = jnp.arange(experts)[None, :] == (first_label + jnp.arange(local))[:, None]

        def up_side(x, gx):
            logits = jnp.einsum("xrd,de->xre", x, router, preferred_element_type=F32)
            gates = jax.nn.softmax(logits, axis=-1)
            gate = jnp.sum(jnp.where(own[:, None, :], gates, 0.0), axis=-1, keepdims=True)
            back = (gate * gx.astype(F32)).astype(BF)
            pre = jnp.einsum("xrd,xdf->xrf", x, expert_up, preferred_element_type=F32)
            hidden, pull = jax.vjp(lambda v: jax.nn.gelu(v, approximate=False), pre)
            hidden = hidden.astype(BF)
            hidden_grad = jnp.einsum("xrd,xfd->xrf", back, expert_down, preferred_element_type=F32)
            pre_grad = pull(hidden_grad)[0].astype(BF)
            return gates, gate, back, hidden, pre_grad

        gates, gate, back, hidden, pre_grad = up_side(x, gx)
        produced = jnp.einsum("xrf,xfd->xrd", hidden, expert_down, preferred_element_type=F32)
        weighted = (gate * produced).astype(BF)
        gate_grad = jnp.sum(gx.astype(F32) * produced, axis=-1, keepdims=True)
        logits_grad = (gates * (jnp.where(own[:, None, :], gate_grad, 0.0) - gate * gate_grad)).astype(BF)
        row_grad = (jnp.einsum("xrf,xdf->xrd", pre_grad, expert_up, preferred_element_type=F32)
                    + jnp.einsum("xre,de->xrd", logits_grad, router, preferred_element_type=F32)).astype(BF)
        router_grad = jnp.einsum("xrd,xre->de", x, logits_grad, preferred_element_type=F32)
        if replicas == 2:
            x2, gx2 = to_expert(swap(rows_in)), to_expert(swap(cot_rows))
            _, _, back2, hidden2, pre_grad2 = up_side(x2, gx2)
            cat = lambda a, b: jnp.concatenate([a, b], axis=1)
        else:
            x2, back2, hidden2, pre_grad2 = x, back, hidden, pre_grad
            cat = lambda a, b: a
        down_grad = jnp.einsum("xrf,xrd->xfd", cat(hidden, hidden2), cat(back, back2), preferred_element_type=F32)
        up_grad = jnp.einsum("xrd,xrf->xdf", cat(x, x2), cat(pre_grad, pre_grad2), preferred_element_type=F32)
        if replicas != 2:
            up_grad, down_grad = lax.psum((up_grad, down_grad), "replica")

        second_rows = come_back(from_expert(row_grad))
        result_rows = come_back(from_expert(weighted))
        second_grad = jnp.einsum("mst,msd->mtd", table, second_rows, preferred_element_type=F32)
        out = (middle + jnp.einsum("mst,msd->mtd", table, result_rows, preferred_element_type=F32)).astype(BF)

        gain_two_grad = jnp.sum(second_grad * hat_two, axis=(0, 1))
        shift_two_grad = jnp.sum(second_grad, axis=(0, 1))
        middle_grad = incoming + norm_back(second_grad, hat_two, inv_two, gain_two)
        branch_grad = middle_grad.astype(BF)
        output_grad = jnp.einsum("mtd,mte->de", mixed, branch_grad, preferred_element_type=F32)
        mixed_grad = jnp.einsum("mte,de->mtd", branch_grad, output, preferred_element_type=F32).astype(BF)
        mixed_grad = mixed_grad.reshape(micro, length, HEADS, HEAD_DIM)
        values_grad = jnp.einsum("mhqk,mqhd->mkhd", probs_low, mixed_grad, preferred_element_type=F32).astype(BF)
        probs_grad = jnp.einsum("mqhd,mkhd->mhqk", mixed_grad, values, preferred_element_type=F32)
        scores_grad = (probs * (probs_grad - jnp.sum(probs * probs_grad, axis=-1, keepdims=True))).astype(BF)
        queries_grad = (jnp.einsum("mhqk,mkhd->mqhd", scores_grad, keys, preferred_element_type=F32) * scale).astype(BF)
        keys_grad = (jnp.einsum("mhqk,mqhd->mkhd", scores_grad, queries, preferred_element_type=F32) * scale).astype(BF)
        joined_grad = jnp.stack([queries_grad, keys_grad, values_grad], axis=2).reshape(micro, length, 3 * width)
        attend_grad = jnp.einsum("mtd,mte->de", normed, joined_grad, preferred_element_type=F32)
        normed_grad = jnp.einsum("mte,de->mtd", joined_grad, attend, preferred_element_type=F32)
        gain_one_grad = jnp.sum(normed_grad * hat_one, axis=(0, 1))
        shift_one_grad = jnp.sum(normed_grad, axis=(0, 1))
        tokens_grad = (middle_grad + norm_back(normed_grad, hat_one, inv_one, gain_one)).astype(BF)

        grads = jnp.concatenate(
            [attend_grad, output_grad, router_grad,
             jnp.stack([gain_one_grad, shift_one_grad, gain_two_grad, shift_two_grad], axis=1)], axis=1).astype(BF)
        grads = jnp.pad(grads, ((0, 0), (0, -cols % 128))).reshape(groups, width // groups, -1)
        grads = lax.all_to_all(grads, "fsdp", split_axis=0, concat_axis=0, tiled=True)
        share = jnp.sum(grads.astype(F32), axis=0)
        share = lax.psum(share, "replica")
        w = 4 * width
        return (out[:, None], tokens_grad[:, None], share[:, w + experts], share[:, w + experts + 1],
                share[:, : 3 * width], share[:, 3 * width : w], share[:, w + experts + 2],
                share[:, w + experts + 3], share[:, w : w + experts], up_grad, down_grad)

    split = ("replica", "fsdp")
    in_specs = (P(None, split), P(None, split), P(None, split), P(), P("fsdp"), P("fsdp"), P("fsdp"), P("fsdp"),
                P("fsdp"), P("fsdp"), P("fsdp"), P("fsdp"), P("fsdp"), P(None, split))
    out_specs = (P(None, split), P(None, split)) + (P("fsdp"),) * 9
    return jax.shard_map(body, mesh=mesh, in_specs=in_specs, out_specs=out_specs, check_vma=False)
```

```python
import functools

import jax
import jax.numpy as jnp
from jax import lax
from jax.experimental import pallas as pl
from jax.experimental.pallas import tpu as pltpu
from jax.sharding import PartitionSpec as P

HEADS = 6
HEAD_DIM = 64
CAP = 16
EPSILON = 1e-06
BF = jnp.bfloat16
F32 = jnp.float32
CHUNKS = 2
TILE = 1536
BLOCK = 256


def dot(a, b, ca, cb):
    return lax.dot_general(a, b, (((ca,), (cb,)), ((), ())), preferred_element_type=F32)


def norm_parts(values):
    center = values - jnp.mean(values, axis=-1, keepdims=True)
    inv = lax.rsqrt(jnp.mean(center * center, axis=-1, keepdims=True) + EPSILON)
    return center * inv, inv


def norm_back(grad, hat, inv, gain):
    scaled = grad * gain
    return inv * (
        scaled
        - jnp.mean(scaled, axis=-1, keepdims=True)
        - hat * jnp.mean(scaled * hat, axis=-1, keepdims=True)
    )


BEND = 0.31
TAIL = (0.12367170304059982, 0.12373026460409164, 0.11044304817914963, 0.09964941442012787,
        0.007125736679881811, 0.1295062005519867, -0.12619934976100922, 0.03207298368215561)

def gelu_pair(v):
    a = 1.0 + BEND * jnp.abs(v)
    k = pl.reciprocal(a, approx=False)
    bell = jnp.exp(v * v * -0.5)
    p = TAIL[7]
    for c in TAIL[6::-1]:
        p = p * k + c
    half = p * k * bell
    phi = jnp.where(v >= 0, 1.0 - half, half)
    return v * phi, phi + v * bell * 0.3989422804014327

def expert_kernel(own, acc, experts, first, local, place_ref, x_ref, g_ref, rt_ref, up_ref, down_ref, *rest):
    rest = list(rest)
    planes = x_ref.shape[0] // 4
    if acc:
        up_in, down_in = rest[:2]; rest = rest[2 + planes :] if own else rest[2:]
    if own:
        w_refs, rest = rest[:planes], rest[planes:]
        rg_ref, ug_ref, dg_ref, og_ref = rest[:4]; rest = rest[4:]
    else:
        ug_ref, dg_ref = rest[:2]; rest = rest[2:]
    if own:
        xt, back, cots, gates_s, hid, pg, prod, rowg = rest
    else:
        xt, back, cots, hid, pg = rest
    e = pl.program_id(0); f = pl.program_id(1)
    nf = pl.num_programs(1)
    R = back.shape[0]
    width = back.shape[1]
    def rows(ref):
        return ref[...].reshape(R, width)
    lane = lax.broadcasted_iota(jnp.int32, (1, 128), 1)
    mine = lane == place_ref[0] * local + first + e

    @pl.when(f == 0)
    def _():
        x = rows(x_ref)
        logits = dot(x, rt_ref[...], 1, 0)
        logits = jnp.where(lane < experts, logits, -1e30)
        top = jnp.max(logits, axis=1, keepdims=True)
        raised = jnp.exp(logits - top)
        gates = raised / jnp.sum(raised, axis=1, keepdims=True)
        gate = jnp.sum(jnp.where(mine, gates, 0.0), axis=1, keepdims=True)
        groups = g_ref.shape[0]
        per = R // groups
        for s in range(groups):
            cots[s * per : (s + 1) * per, :] = g_ref[spot(s ^ place_ref[0], groups // 4)].reshape(per, width)
        back[...] = (gate * cots[...].astype(F32)).astype(BF)
        xt[...] = x.T
        if own:
            gates_s[...] = gates

    x = rows(x_ref)
    step = min(BLOCK, R)
    for b in range(R // step):
        sl = slice(b * step, (b + 1) * step)
        h, d = gelu_pair(dot(x[sl], up_ref[0], 1, 0))
        hid[sl, :] = h.astype(BF)
        pg[sl, :] = (d * dot(back[sl, :], down_ref[0], 1, 1)).astype(BF)
    ug = dot(xt[...], pg[...], 1, 0)
    dg = dot(hid[...], back[...], 0, 0)
    if acc:
        ug = ug + up_in[0]; dg = dg + down_in[0]
    ug_ref[0] = ug
    dg_ref[0] = dg
    if own:
        p = dot(hid[...], down_ref[0], 1, 0)
        r = dot(pg[...], up_ref[0], 1, 1)
        @pl.when(f == 0)
        def _():
            prod[...] = p
            rowg[...] = r
        @pl.when(f > 0)
        def _():
            prod[...] += p
            rowg[...] += r
        @pl.when(f == nf - 1)
        def _():
            gates = gates_s[...]
            gate = jnp.sum(jnp.where(mine, gates, 0.0), axis=1, keepdims=True)
            back[...] = (gate * prod[...]).astype(BF)
            groups = rg_ref.shape[0]
            per = R // groups
            for j in range(groups):
                got = back[pl.ds(pl.multiple_of((j ^ place_ref[0]) * per, per), per), :]
                w_refs[j // 4][j % 4] = got.reshape(w_refs[0].shape[1:])
            gg = jnp.sum(cots[...].astype(F32) * prod[...], axis=1, keepdims=True)
            lg = (gates * (jnp.where(mine, gg, 0.0) - gate * gg)).astype(BF)
            rg_ref[...] = (rowg[...] + dot(lg, rt_ref[...], 1, 1)).astype(BF).reshape(rg_ref.shape)
            og = dot(xt[...], lg, 1, 0)
            @pl.when(e == 0)
            def _():
                og_ref[...] = og
            @pl.when(e > 0)
            def _():
                og_ref[...] += og

def expert_call(own, chunk, micro, place, x, g, full, up, down, experts, acc=None, first=0, span=None, tile=TILE):
    groups, imgs, lc, width = x.shape
    local, _, ff = up.shape
    cap = lc // local
    R = groups * imgs * cap
    span = local if span is None else span
    block = pl.BlockSpec((groups, imgs, cap, width), lambda e, f: (0, 0, e + first, 0))
    wblock = pl.BlockSpec((4, imgs, cap, width), lambda e, f: (0, chunk, e, 0))
    upb = pl.BlockSpec((1, width, tile), lambda e, f: (e + first, 0, f))
    dnb = pl.BlockSpec((1, tile, width), lambda e, f: (e + first, f, 0))
    last = full.shape[1] // 128 - 1
    in_specs = [pl.BlockSpec(memory_space=pltpu.SMEM), block, block,
                pl.BlockSpec((width, 128), lambda e, f: (0, last)), upb, dnb]
    args = [place, x, g, full, up, down]
    alias = {}
    gshape = [jax.ShapeDtypeStruct(up.shape, F32), jax.ShapeDtypeStruct(down.shape, F32)]
    if acc is not None:
        in_specs += [upb, dnb]; args += list(acc[:2])
        if own:
            in_specs += [pl.BlockSpec(memory_space=pl.ANY)] * (groups // 4); args += list(acc[2:])
    out_shape, out_specs = [], []
    if own:
        out_shape += [jax.ShapeDtypeStruct((4, micro, lc, width), BF)] * (groups // 4) + [jax.ShapeDtypeStruct(x.shape, BF)]
        out_specs += [wblock] * (groups // 4) + [block]
    if acc is not None:
        alias = {6: len(out_shape), 7: len(out_shape) + 1}
        if own:
            alias.update({8 + k: k for k in range(groups // 4)})
    out_shape += gshape; out_specs += [upb, dnb]
    if own:
        out_shape.append(jax.ShapeDtypeStruct((width, 128), F32)); out_specs.append(pl.BlockSpec((width, 128), lambda e, f: (0, 0)))
    scratch = [pltpu.VMEM((width, R), BF), pltpu.VMEM((R, width), BF), pltpu.VMEM((R, width), BF)]
    if own: scratch.append(pltpu.VMEM((R, 128), F32))
    scratch += [pltpu.VMEM((R, tile), BF), pltpu.VMEM((R, tile), BF)]
    if own: scratch += [pltpu.VMEM((R, width), F32)] * 2
    return pl.pallas_call(
        functools.partial(expert_kernel, own, acc is not None, experts, first, local),
        grid=(span, ff // tile), in_specs=in_specs, out_specs=out_specs, out_shape=out_shape,
        scratch_shapes=scratch, input_output_aliases=alias,
        cost_estimate=pl.CostEstimate(flops=int(0.7 * (20 if own else 8 * span) * 1.15e9), bytes_accessed=1, transcendentals=0),
        compiler_params=pltpu.CompilerParams(vmem_limit_bytes=56 * 2**20, dimension_semantics=("arbitrary", "arbitrary")),
    )(*args)


def vec_rows(pack_ref, at):
    return pack_ref[:, at:].astype(F32).T


def slot_table(slot_ref, i, slots, at=0):
    rows = lax.broadcasted_iota(jnp.int32, (slots, slot_ref.shape[2]), 0)
    return ((rows == slot_ref[i, at : at + 1, :]) | (rows == slot_ref[i, at + 1 : at + 2, :])).astype(F32).astype(BF)


def spot(j, planes):
    return (j & 1) * (2 * planes) + ((j >> 1) & 1) * planes + (j >> 2)


def route_kernel(experts, place_ref, meta_ref, cap_ref, cot_ref, slot_ref, *rest):
    rows_refs, wide = rest[:-1], rest[-1]
    groups = 4 * len(rows_refs) // CHUNKS
    per = experts * CAP // groups
    images, _, length = meta_ref.shape
    limit_of = cap_ref[...]
    wide[...] = jnp.zeros_like(wide)
    real = cot_ref.shape[2]
    for i in range(images):
        meta = meta_ref[i]
        order = meta[2:3, :]
        earlier = (meta.T[:, 2:3] < order).astype(F32).astype(BF)
        labels = lax.broadcasted_iota(jnp.int32, (experts, length), 0).astype(F32)
        hits = [labels == meta[c : c + 1, :] for c in range(2)]
        ones = [h.astype(F32) for h in hits]
        before = [dot(ones[0].astype(BF), earlier, 1, 0)]
        before.append(dot(ones[1].astype(BF), earlier, 1, 0) + jnp.sum(ones[0], axis=1, keepdims=True))
        for c in range(2):
            position = jnp.sum(ones[c] * before[c], axis=0, keepdims=True)
            limit = jnp.sum(ones[c] * limit_of, axis=0, keepdims=True)
            slot = jnp.where(position < limit, meta[c : c + 1, :] * CAP + position, -1.0)
            slot = slot.astype(jnp.int32)
            slot_ref[i, c : c + 1, :] = slot
            near = slot ^ (place_ref[0] * per)
            slot_ref[i, 2 + c : 3 + c, :] = jnp.where(slot >= 0, near, -1)
            shift = per.bit_length() - 1
            moved = (spot(near >> shift, groups // 4) << shift) + (near & (per - 1))
            slot_ref[i, 4 + c : 5 + c, :] = jnp.where(slot >= 0, moved, -1)
        slot_ref[i, 6:, :] = jnp.full((2, length), -1, jnp.int32)
        wide[i, 0:real, :] = cot_ref[i, 0].astype(F32)
        rows = dot(slot_table(slot_ref, i, experts * CAP, 2), wide[i].astype(BF), 1, 0).astype(BF)
        planes = groups // 4
        count = rows_refs[0].shape[1]
        rows = rows.reshape(planes, 4, per, rows.shape[1])
        for k in range(planes):
            rows_refs[i // count * planes + k][:, i % count] = rows[k]


def route_call(place, meta, limits, cot, size):
    images, _, length = meta.shape
    experts = limits.shape[0]
    width = cot.shape[-1]
    vmem = pl.BlockSpec(memory_space=pltpu.VMEM)
    planes = size // 4
    return pl.pallas_call(
        functools.partial(route_kernel, experts),
        in_specs=[pl.BlockSpec(memory_space=pltpu.SMEM), vmem, vmem, vmem],
        out_shape=[jax.ShapeDtypeStruct((images, 8, length), jnp.int32)]
        + [jax.ShapeDtypeStruct((4, images // CHUNKS, experts * CAP // size, width), BF)] * (planes * CHUNKS),
        scratch_shapes=[pltpu.VMEM((images, length, width), F32)],
        cost_estimate=pl.CostEstimate(flops=2414999999, bytes_accessed=1, transcendentals=0),
        compiler_params=pltpu.CompilerParams(vmem_limit_bytes=48 * 2**20),
    )(place, meta, limits, cot)


def pack_kernel(attend_ref, output_ref, router_ref, vec_ref, out_ref, tall):
    rows, wide = attend_ref.shape
    width = output_ref.shape[1]
    out_ref[:, :wide] = attend_ref[...]
    out_ref[:, wide : wide + width] = output_ref[...]
    tall[...] = jnp.zeros_like(tall)
    experts = router_ref.shape[1]
    tall[0:rows, 0:experts] = router_ref[...].astype(F32)
    vecs = jnp.concatenate([vec_ref[...].astype(F32), jnp.zeros((4, 128), F32)], axis=0)
    turned = jnp.concatenate([vecs] + [jnp.zeros((120, 128), F32)], axis=0).T
    lane = lax.broadcasted_iota(jnp.int32, (128, 128), 1)
    full = jnp.where(lane < experts, tall[...], jnp.roll(turned, experts, axis=1))
    out_ref[:, wide + width :] = full[0:rows].astype(BF)


def half_masks(width):
    lane = lax.broadcasted_iota(jnp.int32, (1, width), 1)
    return [(lane < HEAD_DIM).astype(F32).astype(BF), (lane >= HEAD_DIM).astype(F32).astype(BF)]


def forward_kernel(tok_ref, pack_ref, slot_ref, rows_ref, normed_ref, joined_ref, probs_ref, mixed_ref,
                   middle_ref, wide, heads):
    images, _, real, width = tok_ref.shape
    length = slot_ref.shape[2]
    groups, _, per, _ = rows_ref.shape
    experts = groups * per // CAP
    vecs = vec_rows(pack_ref, 4 * width)[experts : experts + 4]
    gain_one, shift_one, gain_two, shift_two = (vecs[k : k + 1] for k in range(4))
    masks = half_masks(2 * HEAD_DIM)
    key_real = lax.broadcasted_iota(jnp.int32, (1, length), 1) < real
    wide[...] = jnp.zeros_like(wide)
    for i in range(images):
        wide[i, 0:real, :] = tok_ref[i, 0].astype(F32)
        tokens = wide[i]
        hat, _ = norm_parts(tokens)
        normed = (hat * gain_one + shift_one).astype(BF)
        normed_ref[i] = normed
        joined = dot(normed, pack_ref[:, : 3 * width], 1, 0).astype(BF)
        joined_ref[i] = joined
        for pair in range(HEADS // 2):
            at = pair * 2 * HEAD_DIM
            q = joined[:, at : at + 2 * HEAD_DIM] * jnp.asarray(HEAD_DIM ** (-0.5), BF)
            k = joined[:, width + at : width + at + 2 * HEAD_DIM]
            v = joined[:, 2 * width + at : 2 * width + at + 2 * HEAD_DIM]
            both = None
            for s in range(2):
                scores = dot(q * masks[s], k, 1, 1)
                scores = jnp.where(key_real, scores, -1e30)
                raised = jnp.exp(scores - jnp.max(scores, axis=1, keepdims=True))
                probs = raised / jnp.sum(raised, axis=1, keepdims=True)
                probs_ref[i, 2 * pair + s] = probs
                got = dot(probs.astype(BF), v * masks[s], 1, 0)
                both = got if both is None else both + got
            heads[i, :, at : at + 2 * HEAD_DIM] = both.astype(BF)
        mixed = heads[i]
        mixed_ref[i] = mixed
        middle = tokens + dot(mixed, pack_ref[:, 3 * width : 4 * width], 1, 0)
        middle_ref[i] = middle
        hat_two, _ = norm_parts(middle)
        second = (hat_two * gain_two + shift_two).astype(BF)
        rows = dot(slot_table(slot_ref, i, groups * per), second, 1, 0)
        rows_ref[:, i] = rows.astype(BF).reshape(groups, per, width)


def whole(shape):
    return pl.BlockSpec(shape, lambda _: (0,) * len(shape))


def part_of(shape, count, chunk):
    return pl.BlockSpec((count,) + tuple(shape[1:]), lambda _: (chunk,) + (0,) * (len(shape) - 1))


def forward_call(chunk, count, tokens_in, pack, slot, size, slots):
    width = tokens_in.shape[-1]
    length = slot.shape[2]
    shapes = [((size, count, slots // size, width), BF), ((count, length, width), BF), ((count, length, 3 * width), BF),
              ((count, HEADS, length, length), F32), ((count, length, width), BF), ((count, length, width), F32)]
    return pl.pallas_call(
        forward_kernel, grid=(1,),
        in_specs=[part_of(tokens_in.shape, count, chunk), whole(pack.shape),
                  part_of(slot.shape, count, chunk)],
        out_specs=[whole(s) for s, _ in shapes],
        out_shape=[jax.ShapeDtypeStruct(s, d) for s, d in shapes],
        scratch_shapes=[pltpu.VMEM((count, length, width), F32), pltpu.VMEM((count, length, width), BF)],
        cost_estimate=pl.CostEstimate(flops=6440000000, bytes_accessed=1, transcendentals=0),
        compiler_params=pltpu.CompilerParams(vmem_limit_bytes=56 * 2**20),
    )(tokens_in, pack, slot)


def backward_kernel(chunk, acc, last, *refs):
    refs = list(refs)
    (rows_ref, slot_ref, tok_ref, cot_ref, pack_ref, normed_ref, joined_ref, probs_ref, mixed_ref,
     middle_ref) = refs[:10]
    refs = refs[10:]
    if acc:
        attend_in, output_in, vec_in = refs[:3]
        refs = refs[4:]
    if last:
        place_ref, router_in = refs[0], refs[1 : 1 + CHUNKS]
        refs = refs[1 + CHUNKS :]
        grad_ref, keep_ref, send_ref, wide, joined_grad, tall = refs
    else:
        grad_ref, attend_ref, output_ref, vec_ref, wide, joined_grad, tall = refs
    images, _, real, width = tok_ref.shape
    length = slot_ref.shape[2]
    groups, _, per, _ = rows_ref.shape
    experts = groups * per // CAP
    vecs = vec_rows(pack_ref, 4 * width)[experts : experts + 4]
    gain_one, _, gain_two, _ = (vecs[k : k + 1] for k in range(4))
    masks = half_masks(2 * HEAD_DIM)
    scale = HEAD_DIM ** (-0.5)
    attend_sum = output_sum = None
    sums = [None] * 4
    def add(old, new):
        return new if old is None else old + new
    wide[...] = jnp.zeros_like(wide)
    for i in range(images):
        wide[0, i, 0:real, :] = tok_ref[i, 0].astype(F32)
        wide[1, i, 0:real, :] = cot_ref[i, 0].astype(F32)
        table = slot_table(slot_ref, i, groups * per)
        second_grad = dot(table, rows_ref[:, i].reshape(groups * per, width), 0, 0)
        middle = middle_ref[i]
        hat_two, inv_two = norm_parts(middle)
        sums[2] = add(sums[2], jnp.sum(second_grad * hat_two, axis=0, keepdims=True))
        sums[3] = add(sums[3], jnp.sum(second_grad, axis=0, keepdims=True))
        middle_grad = wide[1, i] + norm_back(second_grad, hat_two, inv_two, gain_two)
        branch_grad = middle_grad.astype(BF)
        output_sum = add(output_sum, dot(mixed_ref[i], branch_grad, 0, 0))
        mixed_grad = dot(branch_grad, pack_ref[:, 3 * width : 4 * width], 1, 1).astype(BF)
        joined = joined_ref[i]
        for pair in range(HEADS // 2):
            at = pair * 2 * HEAD_DIM
            q = joined[:, at : at + 2 * HEAD_DIM]
            k = joined[:, width + at : width + at + 2 * HEAD_DIM]
            v = joined[:, 2 * width + at : 2 * width + at + 2 * HEAD_DIM]
            m = mixed_grad[:, at : at + 2 * HEAD_DIM]
            vg = qg = kg = None
            for s in range(2):
                probs = probs_ref[i, 2 * pair + s]
                ms = m * masks[s]
                vg = add(vg, dot(probs.astype(BF), ms, 0, 0))
                probs_grad = dot(ms, v, 1, 1)
                weighed = probs * probs_grad
                scores_grad = (weighed - probs * jnp.sum(weighed, axis=1, keepdims=True)).astype(BF)
                qg = add(qg, dot(scores_grad, k * masks[s], 1, 0))
                kg = add(kg, dot(scores_grad, q * masks[s], 0, 0))
            joined_grad[i, :, at : at + 2 * HEAD_DIM] = (qg * scale).astype(BF)
            joined_grad[i, :, width + at : width + at + 2 * HEAD_DIM] = (kg * scale).astype(BF)
            joined_grad[i, :, 2 * width + at : 2 * width + at + 2 * HEAD_DIM] = vg.astype(BF)
        grads = joined_grad[i]
        attend_sum = add(attend_sum, dot(normed_ref[i], grads, 0, 0))
        normed_grad = dot(grads, pack_ref[:, : 3 * width], 1, 1)
        hat_one, inv_one = norm_parts(wide[0, i])
        sums[0] = add(sums[0], jnp.sum(normed_grad * hat_one, axis=0, keepdims=True))
        sums[1] = add(sums[1], jnp.sum(normed_grad, axis=0, keepdims=True))
        total = (middle_grad + norm_back(normed_grad, hat_one, inv_one, gain_one)).astype(BF)
        grad_ref[i, 0] = total[0:real]
    tall[...] = jnp.zeros_like(tall)
    for k in range(4):
        tall[experts + k : experts + k + 1, :] = sums[k]
    if acc:
        attend_sum = attend_sum + attend_in[...]
        output_sum = output_sum + output_in[...]
    vec = tall[...].T
    if acc:
        vec = vec + vec_in[...]
    if not last:
        attend_ref[...] = attend_sum
        output_ref[...] = output_sum
        vec_ref[...] = vec
        return
    odd = place_ref[0] % 2 == 1
    for part in router_in:
        vec = vec + part[...]
    for value, start in ((attend_sum, 0), (output_sum, 3 * width), (vec, 4 * width)):
        halves = value.reshape(groups // 2, 2, width // groups, value.shape[1])
        zero, one = (halves[:, k].reshape(width // 2, value.shape[1]) for k in range(2))
        at = slice(start, start + value.shape[1])
        keep_ref[:, at] = jnp.where(odd, one, zero)
        send_ref[:, at] = jnp.where(odd, zero, one).astype(BF)


def backward_call(chunk, count, rows, slot, tokens_in, cot, pack, saved, acc, final):
    width = tokens_in.shape[-1]
    length = slot.shape[2]
    args = [rows, slot, tokens_in, cot, pack] + list(saved)
    specs = [whole(rows.shape), part_of(slot.shape, count, chunk), part_of(tokens_in.shape, count, chunk),
             part_of(cot.shape, count, chunk), whole(pack.shape)] + [whole(s.shape) for s in saved]
    sums = [(width, 3 * width), (width, width), (width, 128)]
    alias = {}
    if acc is not None:
        args += list(acc[1:]) + [acc[0]]
        specs += [whole(s) for s in sums] + [pl.BlockSpec(memory_space=pl.ANY)]
        alias = {len(args) - 1: 0}
    kinds = [(s, F32) for s in sums]
    if final is not None:
        args += list(final)
        specs += [pl.BlockSpec(memory_space=pltpu.SMEM)] + [whole(v.shape) for v in final[1:]]
        kinds = [((width // 2, 4 * width + 128), d) for d in (F32, BF)]
    return pl.pallas_call(
        functools.partial(backward_kernel, chunk, acc is not None, final is not None), grid=(1,),
        in_specs=specs, out_specs=[part_of(tokens_in.shape, count, chunk)] + [whole(s) for s, _ in kinds],
        out_shape=[jax.ShapeDtypeStruct(tokens_in.shape, BF)] + [jax.ShapeDtypeStruct(s, d) for s, d in kinds],
        scratch_shapes=[pltpu.VMEM((2, count, length, width), F32), pltpu.VMEM((count, length, 3 * width), BF),
                        pltpu.VMEM((128, width), F32)],
        input_output_aliases=alias,
        cost_estimate=pl.CostEstimate(flops=8855000000, bytes_accessed=1, transcendentals=0),
        compiler_params=pltpu.CompilerParams(vmem_limit_bytes=56 * 2**20),
    )(*args)


def result_kernel(planes, slot_ref, *refs):
    far, side, core, middle, out_ref = refs[:planes], refs[planes], refs[planes + 1], refs[planes + 2 : -1], refs[-1]
    images, real = out_ref.shape[0], out_ref.shape[2]
    _, _, per, width = far[0].shape
    count = middle[0].shape[0]
    for i in range(images):
        rows = [r[0, i] for r in far] + [side[:, 0, i].reshape(planes * per, width)]
        rows = jnp.concatenate(rows + [core[:, i].reshape(2 * planes * per, width)], axis=0)
        table = slot_table(slot_ref, i, rows.shape[0], 4)
        out = middle[i // count][i % count] + dot(table, rows, 0, 0)
        out_ref[i, 0] = out.astype(BF)[0:real]


def result_call(far, side, core, slot, middle, shape):
    return pl.pallas_call(
        functools.partial(result_kernel, len(far)), out_shape=jax.ShapeDtypeStruct(shape, BF),
        cost_estimate=pl.CostEstimate(flops=2414999999, bytes_accessed=1, transcendentals=0),
        compiler_params=pltpu.CompilerParams(vmem_limit_bytes=32 * 2**20),
    )(slot, *far, side, core, *middle)


def flips(size, bit):
    return [(i, i ^ bit) for i in range(size)]


def in_order(parts, index):
    while len(parts) > 1:
        half = len(parts) // 2
        high = (index // half) % 2 == 1
        low, top = parts[:half], parts[half:]
        parts_low = [jnp.where(high, t, l) for l, t in zip(low, top)]
        parts_top = [jnp.where(high, l, t) for l, t in zip(low, top)]
        index = index % half
        if half == 1:
            return [parts_low[0], parts_top[0]]
        return in_order(parts_low, index) + in_order(parts_top, index)
    return parts


def hop(v, size, bit):
    return lax.ppermute(v, "fsdp", flips(size, bit))


def gather_far(piece, size):
    far = [piece] + [hop(piece, size, 4 * k) for k in range(1, size // 4)]
    return jnp.stack(in_order(far, lax.axis_index("fsdp") // 4))


def gather_near(held, size, bit):
    came = hop(held, size, bit)
    axis = 1 if bit == 2 else 2
    mine = (lax.axis_index("fsdp") // bit) % 2
    side = lax.broadcasted_iota(jnp.int32, held.shape[:axis] + (2,) + held.shape[axis:], axis)
    return jnp.where(side == mine, jnp.expand_dims(held, axis), jnp.expand_dims(came, axis))


def side_hop(far, size):
    return hop(jnp.stack([p[2:4] for p in far]), size, 2)


def core_hop(far, side, size):
    return hop(jnp.concatenate([jnp.stack([p[1] for p in far]), side[:, 1]]), size, 1)


def joined_pieces(far, side, core):
    return jnp.concatenate([jnp.stack([p[0] for p in far]), side[:, 0], core])


def after(value, *others):
    return lax.optimization_barrier((value,) + others)[0]


def scatter_sum(keep, send, size, replicas, between, *wait):
    index = lax.axis_index("fsdp")
    planes = size // 4
    held = keep + hop(send, size, 1).astype(F32)
    rows = held.shape[0] // (planes * 2)
    held = held.reshape(planes, 2, rows, -1)
    high = (index // 2) % 2 == 1
    gone = jnp.where(high, held[:, 0], held[:, 1]).astype(BF)
    between[0](gone)
    came = hop(after(gone, *wait), size, 2)
    held = jnp.where(high, held[:, 1], held[:, 0]) + came.astype(F32)
    low = held.astype(BF)
    place = index // 4
    total = lax.dynamic_index_in_dim(held, place, 0, keepdims=False)
    gone = [lax.dynamic_index_in_dim(low, place ^ k, 0, keepdims=False) for k in range(1, planes)]
    between[1](gone[0])
    for k in range(1, planes):
        total = total + hop(gone[k - 1], size, 4 * k).astype(F32)
    if replicas == 2:
        low = total.astype(BF)
        between[2](low)
        return low.astype(F32) + lax.ppermute(low, "replica", [(0, 1), (1, 0)]).astype(F32)
    return lax.psum(total, "replica")


def solution(mesh):
    replicas = mesh.shape["replica"]
    size = mesh.shape["fsdp"]

    def body(tokens_in, picks_in, ranks_in, capacity, first_gain, first_shift, attend_weight,
             output_weight, second_gain, second_shift, router_weight, expert_up, expert_down, cotangent):
        micro, _, length, width = tokens_in.shape
        experts = capacity.shape[0]
        slots = experts * CAP
        tall = -(-length // 128) * 128
        share = attend_weight.shape[0]
        vecs = jnp.stack([first_gain, first_shift, second_gain, second_shift])
        vecs = jnp.pad(vecs, ((0, 0), (0, 128 - share)))
        packed = pl.pallas_call(
            pack_kernel, out_shape=jax.ShapeDtypeStruct((share, 4 * width + 128), BF),
            cost_estimate=pl.CostEstimate(flops=1610000000, bytes_accessed=1, transcendentals=0),
        scratch_shapes=[pltpu.VMEM((128, 128), F32)],
        )(attend_weight, output_weight, router_weight, vecs)
        far = gather_far(packed, size)

        place = lax.axis_index("fsdp").astype(jnp.int32).reshape(1)
        meta = jnp.concatenate([picks_in[:, 0].transpose(0, 2, 1), ranks_in], axis=1).astype(F32)
        meta = jnp.pad(meta, ((0, 0), (0, 5), (0, tall - length)), constant_values=1000.0)
        slot, *cot_out = route_call(place, meta, capacity.astype(F32)[:, None], cotangent, size)
        count = micro // CHUNKS
        chunks = range(CHUNKS)
        near = gather_near(after(far, slot), size, 2)
        planes = size // 4
        cot_far = []
        for c in chunks:
            first = far if c == 0 else cot_far[c - 1][1]
            ready = lax.optimization_barrier((first, *cot_out[c * planes : (c + 1) * planes]))[1:]
            cot_far.append([q if k == 0 else hop(q, size, 4 * k) for k, q in enumerate(ready)])
        full = gather_near(near, size, 1).reshape(size * share, -1)

        def exchange(r):
            return lax.all_to_all(r, "fsdp", split_axis=0, concat_axis=0, tiled=True)

        def swap(v):
            return lax.ppermute(v, "replica", [(0, 1), (1, 0)])

        rows_in, cot_rows, saved = [], [], []
        for c in chunks:
            sent, *kept = forward_call(c, count, tokens_in, full, slot, size, slots)
            rows_in.append(exchange(after(sent, *cot_far[c])))
            saved.append(kept)
            arrived = lax.optimization_barrier((sent, *cot_far[c]))[1:]
            side = side_hop(arrived, size)
            cot_rows.append(joined_pieces(arrived, side, core_hop(arrived, side, size)))
        paired = replicas == 2
        swapped = [(swap(g), swap(x)) if paired else () for x, g in zip(rows_in, cot_rows)]

        acc = None
        row_grads, router_grads = [], []
        for c in chunks:
            wait = swapped[c - 1] if c > 0 else ()
            *w, r, ug, dg, og = expert_call(True, c, micro, after(place, *wait), rows_in[c], cot_rows[c], full,
                                            expert_up, expert_down, experts, acc)
            acc = (ug, dg, *w)
            row_grads.append(exchange(r))
            router_grads.append(og)
        acc, result_far = acc[:2], acc[2:]
        result_far = [q if k == 0 else hop(q, size, 4 * k) for k, q in enumerate(result_far)]
        sums = None
        box = [acc]

        def other(c, first, span, *wait):
            if paired:
                g, x = swapped[c]
                box[0] = expert_call(False, c, micro, after(place, *wait), x, g, full,
                                     expert_up, expert_down, experts, box[0], first, span)

        for c in chunks:
            last = c == CHUNKS - 1
            final = (after(place, box[0][0]), *router_grads) if last else None
            slots_in = after(slot, *swapped[-1]) if last else slot
            sums = backward_call(c, count, row_grads[c], slots_in, tokens_in, cotangent, full, saved[c], sums, final)
            if not last:
                other(c, 0, None, sums[1])
                result_far = lax.optimization_barrier((box[0][0], *result_far))[1:]
                result_side = side_hop(result_far, size)
        token_grad, keep, send = sums
        local = expert_up.shape[0]
        tail = []
        total = scatter_sum(keep, send, size, replicas, (lambda gone: other(CHUNKS - 1, 0, local // 2, gone),
                                                         lambda gone: other(CHUNKS - 1, local // 2, local // 2, gone),
                                                         tail.append), result_side)
        acc = box[0]
        if not paired:
            acc = lax.psum(tuple(acc), "replica")
        up_grad, down_grad = acc
        out = result_call(result_far, result_side, core_hop(result_far, result_side, size), after(slot, *tail),
                          [s[4] for s in saved], tokens_in.shape)

        w = 4 * width + experts
        return (out, token_grad, total[:, w], total[:, w + 1], total[:, : 3 * width], total[:, 3 * width : 4 * width],
                total[:, w + 2], total[:, w + 3], total[:, 4 * width : w], up_grad, down_grad)

    split = ("replica", "fsdp")
    in_specs = (P(None, split), P(None, split), P(None, split), P(), P("fsdp"), P("fsdp"), P("fsdp"), P("fsdp"),
                P("fsdp"), P("fsdp"), P("fsdp"), P("fsdp"), P("fsdp"), P(None, split))
    out_specs = (P(None, split), P(None, split)) + (P("fsdp"),) * 9
    return jax.shard_map(body, mesh=mesh, in_specs=in_specs, out_specs=out_specs, check_vma=False)
```

```python
import functools

import jax
import jax.numpy as jnp
from jax import lax
from jax.experimental import pallas as pl
from jax.experimental.pallas import tpu as pltpu
from jax.sharding import PartitionSpec as P

HEADS = 6
HEAD_DIM = 64
CAP = 16
EPSILON = 1e-06
BF = jnp.bfloat16
F32 = jnp.float32
CHUNKS = 2
F1, F2, F3, F4, F5, F6, F7, F8, F9 = 1, 2, 1, 0, 1, 3, 0, 0, 1
TILE = 1536
BLOCK = 256


def dot(a, b, ca, cb):
    return lax.dot_general(a, b, (((ca,), (cb,)), ((), ())), preferred_element_type=F32)


def norm_parts(values):
    center = values - jnp.mean(values, axis=-1, keepdims=True)
    inv = lax.rsqrt(jnp.mean(center * center, axis=-1, keepdims=True) + EPSILON)
    return center * inv, inv


def norm_back(grad, hat, inv, gain):
    scaled = grad * gain
    return inv * (
        scaled
        - jnp.mean(scaled, axis=-1, keepdims=True)
        - hat * jnp.mean(scaled * hat, axis=-1, keepdims=True)
    )


BEND = 0.31
TAIL = (0.12367170304059982, 0.12373026460409164, 0.11044304817914963, 0.09964941442012787,
        0.007125736679881811, 0.1295062005519867, -0.12619934976100922, 0.03207298368215561)

def gelu_pair(v):
    a = 1.0 + BEND * jnp.abs(v)
    k = pl.reciprocal(a, approx=False)
    bell = jnp.exp(v * v * -0.5)
    p = TAIL[7]
    for c in TAIL[6::-1]:
        p = p * k + c
    half = p * k * bell
    phi = jnp.where(v >= 0, 1.0 - half, half)
    return v * phi, phi + v * bell * 0.3989422804014327

def expert_kernel(own, acc, experts, first, local, planes, place_ref, rt_ref, up_ref, down_ref, *rest):
    rest = list(rest)

    def take(n):
        got = rest[:n]
        del rest[:n]
        return got

    x_refs = take(1 if own else CHUNKS)
    g_refs = take(planes + 2 if own else CHUNKS)
    if acc:
        up_in, down_in = take(2)
        if own:
            take(2)
    if own:
        w_refs = take(2)
        rg_ref, cot_ref = take(2)
    ug_ref, dg_ref = take(2)
    if own:
        og_ref, = take(1)
        xt, back, cots, gates_s, hid, pg, prod, rowg = rest
    else:
        xt, back, cots, xs, hid, pg = rest
    e = pl.program_id(0); f = pl.program_id(1)
    nf = pl.num_programs(1)
    R = back.shape[0]
    width = back.shape[1]
    groups = 4 * planes
    def rows(refs):
        return jnp.concatenate([r[...].reshape(R // len(refs), width) for r in refs], axis=0)
    lane = lax.broadcasted_iota(jnp.int32, (1, 128), 1)
    mine = lane == place_ref[0] * local + first + e

    @pl.when(f == 0)
    def _():
        x = rows(x_refs)
        if not own:
            xs[...] = x
        logits = dot(x, rt_ref[...], 1, 0)
        logits = jnp.where(lane < experts, logits, -1e30)
        top = jnp.max(logits, axis=1, keepdims=True)
        raised = jnp.exp(logits - top)
        gates = raised / jnp.sum(raised, axis=1, keepdims=True)
        gate = jnp.sum(jnp.where(mine, gates, 0.0), axis=1, keepdims=True)
        if own:
            per = R // groups
            side, core = g_refs[planes:]
            for k in range(planes):
                for j, got in ((0, g_refs[k][0]), (2, side[k, 0]), (1, core[k]), (3, core[planes + k])):
                    at = pl.multiple_of(((4 * k + j) ^ place_ref[0]) * per, per)
                    cots[pl.ds(at, per), :] = got.reshape(per, width)
            cot_ref[...] = cots[...].reshape(cot_ref.shape)
        else:
            cots[...] = rows(g_refs)
        back[...] = (gate * cots[...].astype(F32)).astype(BF)
        xt[...] = x.T
        if own:
            gates_s[...] = gates

    x = rows(x_refs) if own else xs[...]
    step = min(BLOCK, R)
    for b in range(R // step):
        sl = slice(b * step, (b + 1) * step)
        h, d = gelu_pair(dot(x[sl], up_ref[0], 1, 0))
        hid[sl, :] = h.astype(BF)
        pg[sl, :] = (d * dot(back[sl, :], down_ref[0], 1, 1)).astype(BF)
    ug = dot(xt[...], pg[...], 1, 0)
    dg = dot(hid[...], back[...], 0, 0)
    if acc:
        ug = ug + up_in[0]; dg = dg + down_in[0]
    ug_ref[0] = ug
    dg_ref[0] = dg
    if own:
        p = dot(hid[...], down_ref[0], 1, 0)
        r = dot(pg[...], up_ref[0], 1, 1)
        @pl.when(f == 0)
        def _():
            prod[...] = p
            rowg[...] = r
        @pl.when(f > 0)
        def _():
            prod[...] += p
            rowg[...] += r
        @pl.when(f == nf - 1)
        def _():
            gates = gates_s[...]
            gate = jnp.sum(jnp.where(mine, gates, 0.0), axis=1, keepdims=True)
            back[...] = (gate * prod[...]).astype(BF)
            per = R // groups
            for j in range(groups):
                got = back[pl.ds(pl.multiple_of((j ^ place_ref[0]) * per, per), per), :]
                w_refs[j // 2 % 2][j // 4, j % 2] = got.reshape(w_refs[0].shape[2:])
            gg = jnp.sum(cots[...].astype(F32) * prod[...], axis=1, keepdims=True)
            lg = (gates * (jnp.where(mine, gg, 0.0) - gate * gg)).astype(BF)
            rg_ref[...] = (rowg[...] + dot(lg, rt_ref[...], 1, 1)).astype(BF).reshape(rg_ref.shape)
            og = dot(xt[...], lg, 1, 0)
            @pl.when(e == 0)
            def _():
                og_ref[...] = og
            @pl.when(e > 0)
            def _():
                og_ref[...] += og

def expert_call(own, chunk, micro, place, xs, gs, full, up, down, experts, acc=None, first=0, span=None, tile=TILE):
    groups, imgs, lc, width = xs[0].shape
    local, _, ff = up.shape
    cap = lc // local
    planes = groups // 4
    R = groups * imgs * cap * len(xs)
    span = local if span is None else span
    block = pl.BlockSpec((groups, imgs, cap, width), lambda e, f: (0, 0, e + first, 0))
    upb = pl.BlockSpec((1, width, tile), lambda e, f: (e + first, 0, f))
    dnb = pl.BlockSpec((1, tile, width), lambda e, f: (e + first, f, 0))
    last = full.shape[1] // 128 - 1
    in_specs = [pl.BlockSpec(memory_space=pltpu.SMEM), pl.BlockSpec((width, 128), lambda e, f: (0, last)), upb, dnb]
    in_specs += [block] * len(xs)
    if own:
        in_specs += [pl.BlockSpec((1, imgs, cap, width), lambda e, f: (0, 0, e, 0))] * planes
        in_specs += [pl.BlockSpec((planes, 1, imgs, cap, width), lambda e, f: (0, 0, 0, e, 0)),
                     pl.BlockSpec((2 * planes, imgs, cap, width), lambda e, f: (0, 0, e, 0))]
    else:
        in_specs += [block] * len(gs)
    args = [place, full, up, down, *xs, *gs]
    out_shape, out_specs, alias = [], [], {}
    if own:
        out_shape += [jax.ShapeDtypeStruct((planes, 2, micro, lc, width), BF)] * 2
        out_shape += [jax.ShapeDtypeStruct(xs[0].shape, BF)] * 2
        out_specs += [pl.BlockSpec((planes, 2, imgs, cap, width), lambda e, f: (0, 0, chunk, e, 0))] * 2 + [block] * 2
    if acc is not None:
        at = len(args)
        alias = {at: len(out_shape), at + 1: len(out_shape) + 1}
        in_specs += [upb, dnb]
        args += list(acc[:2])
        if own:
            alias.update({at + 2: 0, at + 3: 1})
            in_specs += [pl.BlockSpec(memory_space=pl.ANY)] * 2
            args += list(acc[2:])
    out_shape += [jax.ShapeDtypeStruct(up.shape, F32), jax.ShapeDtypeStruct(down.shape, F32)]
    out_specs += [upb, dnb]
    scratch = [pltpu.VMEM((width, R), BF), pltpu.VMEM((R, width), BF), pltpu.VMEM((R, width), BF)]
    if own:
        out_shape.append(jax.ShapeDtypeStruct((width, 128), F32))
        out_specs.append(pl.BlockSpec((width, 128), lambda e, f: (0, 0)))
        scratch.append(pltpu.VMEM((R, 128), F32))
    else:
        scratch.append(pltpu.VMEM((R, width), BF))
    scratch += [pltpu.VMEM((R, tile), BF), pltpu.VMEM((R, tile), BF)]
    if own:
        scratch += [pltpu.VMEM((R, width), F32)] * 2
    return pl.pallas_call(
        functools.partial(expert_kernel, own, acc is not None, experts, first, local, planes),
        grid=(span, ff // tile), in_specs=in_specs, out_specs=out_specs, out_shape=out_shape,
        scratch_shapes=scratch, input_output_aliases=alias,
        cost_estimate=pl.CostEstimate(flops=int((20 * 1.5 if own else 15 * 0.7 * span) * 1.15e9), bytes_accessed=1, transcendentals=0),
        compiler_params=pltpu.CompilerParams(vmem_limit_bytes=56 * 2**20, dimension_semantics=("arbitrary", "arbitrary")),
    )(*args)


def vec_rows(pack_ref, at):
    return pack_ref[:, at:].astype(F32).T


def slot_table(slot_ref, i, slots, at=0):
    rows = lax.broadcasted_iota(jnp.int32, (slots, slot_ref.shape[2]), 0)
    return ((rows == slot_ref[i, at : at + 1, :]) | (rows == slot_ref[i, at + 1 : at + 2, :])).astype(F32).astype(BF)


def spot(j, planes):
    return (j & 1) * (2 * planes) + (j >> 1)


def route_kernel(experts, place_ref, meta_ref, cap_ref, cot_ref, slot_ref, *rest):
    rows_refs, wide = rest[:-1], rest[-1]
    groups = 4 * len(rows_refs) // CHUNKS
    per = experts * CAP // groups
    images, _, length = meta_ref.shape
    limit_of = cap_ref[...]
    wide[...] = jnp.zeros_like(wide)
    real = cot_ref.shape[2]
    for i in range(images):
        meta = meta_ref[i]
        order = meta[2:3, :]
        earlier = (meta.T[:, 2:3] < order).astype(F32).astype(BF)
        labels = lax.broadcasted_iota(jnp.int32, (experts, length), 0).astype(F32)
        hits = [labels == meta[c : c + 1, :] for c in range(2)]
        ones = [h.astype(F32) for h in hits]
        before = [dot(ones[0].astype(BF), earlier, 1, 0)]
        before.append(dot(ones[1].astype(BF), earlier, 1, 0) + jnp.sum(ones[0], axis=1, keepdims=True))
        for c in range(2):
            position = jnp.sum(ones[c] * before[c], axis=0, keepdims=True)
            limit = jnp.sum(ones[c] * limit_of, axis=0, keepdims=True)
            slot = jnp.where(position < limit, meta[c : c + 1, :] * CAP + position, -1.0)
            slot = slot.astype(jnp.int32)
            slot_ref[i, c : c + 1, :] = slot
            near = slot ^ (place_ref[0] * per)
            slot_ref[i, 2 + c : 3 + c, :] = jnp.where(slot >= 0, near, -1)
            shift = per.bit_length() - 1
            moved = (spot(near >> shift, groups // 4) << shift) + (near & (per - 1))
            slot_ref[i, 4 + c : 5 + c, :] = jnp.where(slot >= 0, moved, -1)
        slot_ref[i, 6:, :] = jnp.full((2, length), -1, jnp.int32)
        wide[i, 0:real, :] = cot_ref[i, 0].astype(F32)
        rows = dot(slot_table(slot_ref, i, experts * CAP, 2), wide[i].astype(BF), 1, 0).astype(BF)
        planes = groups // 4
        count = rows_refs[0].shape[1]
        rows = rows.reshape(planes, 4, per, rows.shape[1])
        for k in range(planes):
            rows_refs[i // count * planes + k][:, i % count] = rows[k]


def route_call(place, meta, limits, cot, size):
    images, _, length = meta.shape
    experts = limits.shape[0]
    width = cot.shape[-1]
    vmem = pl.BlockSpec(memory_space=pltpu.VMEM)
    planes = size // 4
    return pl.pallas_call(
        functools.partial(route_kernel, experts),
        in_specs=[pl.BlockSpec(memory_space=pltpu.SMEM), vmem, vmem, vmem],
        out_shape=[jax.ShapeDtypeStruct((images, 8, length), jnp.int32)]
        + [jax.ShapeDtypeStruct((4, images // CHUNKS, experts * CAP // size, width), BF)] * (planes * CHUNKS),
        scratch_shapes=[pltpu.VMEM((images, length, width), F32)],
        cost_estimate=pl.CostEstimate(flops=3450000000, bytes_accessed=1, transcendentals=0),
        compiler_params=pltpu.CompilerParams(vmem_limit_bytes=48 * 2**20),
    )(place, meta, limits, cot)


def pack_kernel(attend_ref, output_ref, router_ref, vec_ref, out_ref, tall):
    rows, wide = attend_ref.shape
    width = output_ref.shape[1]
    out_ref[:, :wide] = attend_ref[...]
    out_ref[:, wide : wide + width] = output_ref[...]
    tall[...] = jnp.zeros_like(tall)
    experts = router_ref.shape[1]
    tall[0:rows, 0:experts] = router_ref[...].astype(F32)
    vecs = jnp.concatenate([vec_ref[...].astype(F32), jnp.zeros((4, 128), F32)], axis=0)
    turned = jnp.concatenate([vecs] + [jnp.zeros((120, 128), F32)], axis=0).T
    lane = lax.broadcasted_iota(jnp.int32, (128, 128), 1)
    full = jnp.where(lane < experts, tall[...], jnp.roll(turned, experts, axis=1))
    out_ref[:, wide + width :] = full[0:rows].astype(BF)


def half_masks(width):
    lane = lax.broadcasted_iota(jnp.int32, (1, width), 1)
    return [(lane < HEAD_DIM).astype(F32).astype(BF), (lane >= HEAD_DIM).astype(F32).astype(BF)]


def forward_kernel(tok_ref, pack_ref, slot_ref, rows_ref, normed_ref, joined_ref, probs_ref, mixed_ref,
                   middle_ref, wide, heads):
    images, _, real, width = tok_ref.shape
    length = slot_ref.shape[2]
    groups, _, per, _ = rows_ref.shape
    experts = groups * per // CAP
    vecs = vec_rows(pack_ref, 4 * width)[experts : experts + 4]
    gain_one, shift_one, gain_two, shift_two = (vecs[k : k + 1] for k in range(4))
    masks = half_masks(2 * HEAD_DIM)
    key_real = lax.broadcasted_iota(jnp.int32, (1, length), 1) < real
    wide[...] = jnp.zeros_like(wide)
    for i in range(images):
        wide[i, 0:real, :] = tok_ref[i, 0].astype(F32)
        tokens = wide[i]
        hat, _ = norm_parts(tokens)
        normed = (hat * gain_one + shift_one).astype(BF)
        normed_ref[i] = normed
        joined = dot(normed, pack_ref[:, : 3 * width], 1, 0).astype(BF)
        joined_ref[i] = joined
        for pair in range(HEADS // 2):
            at = pair * 2 * HEAD_DIM
            q = joined[:, at : at + 2 * HEAD_DIM] * jnp.asarray(HEAD_DIM ** (-0.5), BF)
            k = joined[:, width + at : width + at + 2 * HEAD_DIM]
            v = joined[:, 2 * width + at : 2 * width + at + 2 * HEAD_DIM]
            both = None
            for s in range(2):
                scores = dot(q * masks[s], k, 1, 1)
                scores = jnp.where(key_real, scores, -1e30)
                raised = jnp.exp(scores - jnp.max(scores, axis=1, keepdims=True))
                probs = raised / jnp.sum(raised, axis=1, keepdims=True)
                probs_ref[i, 2 * pair + s] = probs
                got = dot(probs.astype(BF), v * masks[s], 1, 0)
                both = got if both is None else both + got
            heads[i, :, at : at + 2 * HEAD_DIM] = both.astype(BF)
        mixed = heads[i]
        mixed_ref[i] = mixed
        middle = tokens + dot(mixed, pack_ref[:, 3 * width : 4 * width], 1, 0)
        middle_ref[i] = middle
        hat_two, _ = norm_parts(middle)
        second = (hat_two * gain_two + shift_two).astype(BF)
        rows = dot(slot_table(slot_ref, i, groups * per), second, 1, 0)
        rows_ref[:, i] = rows.astype(BF).reshape(groups, per, width)


def whole(shape):
    return pl.BlockSpec(shape, lambda _: (0,) * len(shape))


def part_of(shape, count, chunk):
    return pl.BlockSpec((count,) + tuple(shape[1:]), lambda _: (chunk,) + (0,) * (len(shape) - 1))


def forward_call(chunk, count, tokens_in, pack, slot, size, slots):
    width = tokens_in.shape[-1]
    length = slot.shape[2]
    shapes = [((size, count, slots // size, width), BF), ((count, length, width), BF), ((count, length, 3 * width), BF),
              ((count, HEADS, length, length), F32), ((count, length, width), BF), ((count, length, width), F32)]
    return pl.pallas_call(
        forward_kernel, grid=(1,),
        in_specs=[part_of(tokens_in.shape, count, chunk), whole(pack.shape),
                  part_of(slot.shape, count, chunk)],
        out_specs=[whole(s) for s, _ in shapes],
        out_shape=[jax.ShapeDtypeStruct(s, d) for s, d in shapes],
        scratch_shapes=[pltpu.VMEM((count, length, width), F32), pltpu.VMEM((count, length, width), BF)],
        cost_estimate=pl.CostEstimate(flops=6440000000, bytes_accessed=1, transcendentals=0),
        compiler_params=pltpu.CompilerParams(vmem_limit_bytes=56 * 2**20),
    )(tokens_in, pack, slot)


def backward_kernel(chunk, acc, last, *refs):
    refs = list(refs)
    (rows_ref, slot_ref, tok_ref, cot_ref, pack_ref, normed_ref, joined_ref, probs_ref, mixed_ref,
     middle_ref) = refs[:10]
    refs = refs[10:]
    if acc:
        attend_in, output_in, vec_in = refs[:3]
        refs = refs[4:]
    if last:
        place_ref, router_in = refs[0], refs[1 : 1 + CHUNKS]
        refs = refs[1 + CHUNKS :]
        grad_ref, keep_ref, send_ref, wide, joined_grad, tall = refs
    else:
        grad_ref, attend_ref, output_ref, vec_ref, wide, joined_grad, tall = refs
    images, _, real, width = tok_ref.shape
    length = slot_ref.shape[2]
    groups, _, per, _ = rows_ref.shape
    experts = groups * per // CAP
    vecs = vec_rows(pack_ref, 4 * width)[experts : experts + 4]
    gain_one, _, gain_two, _ = (vecs[k : k + 1] for k in range(4))
    masks = half_masks(2 * HEAD_DIM)
    scale = HEAD_DIM ** (-0.5)
    attend_sum = output_sum = None
    sums = [None] * 4
    def add(old, new):
        return new if old is None else old + new
    wide[...] = jnp.zeros_like(wide)
    for i in range(images):
        wide[0, i, 0:real, :] = tok_ref[i, 0].astype(F32)
        wide[1, i, 0:real, :] = cot_ref[i, 0].astype(F32)
        table = slot_table(slot_ref, i, groups * per)
        second_grad = dot(table, rows_ref[:, i].reshape(groups * per, width), 0, 0)
        middle = middle_ref[i]
        hat_two, inv_two = norm_parts(middle)
        sums[2] = add(sums[2], jnp.sum(second_grad * hat_two, axis=0, keepdims=True))
        sums[3] = add(sums[3], jnp.sum(second_grad, axis=0, keepdims=True))
        middle_grad = wide[1, i] + norm_back(second_grad, hat_two, inv_two, gain_two)
        branch_grad = middle_grad.astype(BF)
        output_sum = add(output_sum, dot(mixed_ref[i], branch_grad, 0, 0))
        mixed_grad = dot(branch_grad, pack_ref[:, 3 * width : 4 * width], 1, 1).astype(BF)
        joined = joined_ref[i]
        for pair in range(HEADS // 2):
            at = pair * 2 * HEAD_DIM
            q = joined[:, at : at + 2 * HEAD_DIM]
            k = joined[:, width + at : width + at + 2 * HEAD_DIM]
            v = joined[:, 2 * width + at : 2 * width + at + 2 * HEAD_DIM]
            m = mixed_grad[:, at : at + 2 * HEAD_DIM]
            vg = qg = kg = None
            for s in range(2):
                probs = probs_ref[i, 2 * pair + s]
                ms = m * masks[s]
                vg = add(vg, dot(probs.astype(BF), ms, 0, 0))
                probs_grad = dot(ms, v, 1, 1)
                weighed = probs * probs_grad
                scores_grad = (weighed - probs * jnp.sum(weighed, axis=1, keepdims=True)).astype(BF)
                qg = add(qg, dot(scores_grad, k * masks[s], 1, 0))
                kg = add(kg, dot(scores_grad, q * masks[s], 0, 0))
            joined_grad[i, :, at : at + 2 * HEAD_DIM] = (qg * scale).astype(BF)
            joined_grad[i, :, width + at : width + at + 2 * HEAD_DIM] = (kg * scale).astype(BF)
            joined_grad[i, :, 2 * width + at : 2 * width + at + 2 * HEAD_DIM] = vg.astype(BF)
        grads = joined_grad[i]
        attend_sum = add(attend_sum, dot(normed_ref[i], grads, 0, 0))
        normed_grad = dot(grads, pack_ref[:, : 3 * width], 1, 1)
        hat_one, inv_one = norm_parts(wide[0, i])
        sums[0] = add(sums[0], jnp.sum(normed_grad * hat_one, axis=0, keepdims=True))
        sums[1] = add(sums[1], jnp.sum(normed_grad, axis=0, keepdims=True))
        total = (middle_grad + norm_back(normed_grad, hat_one, inv_one, gain_one)).astype(BF)
        grad_ref[i, 0] = total[0:real]
    tall[...] = jnp.zeros_like(tall)
    for k in range(4):
        tall[experts + k : experts + k + 1, :] = sums[k]
    if acc:
        attend_sum = attend_sum + attend_in[...]
        output_sum = output_sum + output_in[...]
    vec = tall[...].T
    if acc:
        vec = vec + vec_in[...]
    if not last:
        attend_ref[...] = attend_sum
        output_ref[...] = output_sum
        vec_ref[...] = vec
        return
    odd = place_ref[0] % 2 == 1
    for part in router_in:
        vec = vec + part[...]
    for value, start in ((attend_sum, 0), (output_sum, 3 * width), (vec, 4 * width)):
        halves = value.reshape(groups // 2, 2, width // groups, value.shape[1])
        zero, one = (halves[:, k].reshape(width // 2, value.shape[1]) for k in range(2))
        at = slice(start, start + value.shape[1])
        keep_ref[:, at] = jnp.where(odd, one, zero)
        send_ref[:, at] = jnp.where(odd, zero, one).astype(BF)


def backward_call(chunk, count, rows, slot, tokens_in, cot, pack, saved, acc, final):
    width = tokens_in.shape[-1]
    length = slot.shape[2]
    args = [rows, slot, tokens_in, cot, pack] + list(saved)
    specs = [whole(rows.shape), part_of(slot.shape, count, chunk), part_of(tokens_in.shape, count, chunk),
             part_of(cot.shape, count, chunk), whole(pack.shape)] + [whole(s.shape) for s in saved]
    sums = [(width, 3 * width), (width, width), (width, 128)]
    alias = {}
    if acc is not None:
        args += list(acc[1:]) + [acc[0]]
        specs += [whole(s) for s in sums] + [pl.BlockSpec(memory_space=pl.ANY)]
        alias = {len(args) - 1: 0}
    kinds = [(s, F32) for s in sums]
    if final is not None:
        args += list(final)
        specs += [pl.BlockSpec(memory_space=pltpu.SMEM)] + [whole(v.shape) for v in final[1:]]
        kinds = [((width // 2, 4 * width + 128), d) for d in (F32, BF)]
    return pl.pallas_call(
        functools.partial(backward_kernel, chunk, acc is not None, final is not None), grid=(1,),
        in_specs=specs, out_specs=[part_of(tokens_in.shape, count, chunk)] + [whole(s) for s, _ in kinds],
        out_shape=[jax.ShapeDtypeStruct(tokens_in.shape, BF)] + [jax.ShapeDtypeStruct(s, d) for s, d in kinds],
        scratch_shapes=[pltpu.VMEM((2, count, length, width), F32), pltpu.VMEM((count, length, 3 * width), BF),
                        pltpu.VMEM((128, width), F32)],
        input_output_aliases=alias,
        cost_estimate=pl.CostEstimate(flops=8855000000, bytes_accessed=1, transcendentals=0),
        compiler_params=pltpu.CompilerParams(vmem_limit_bytes=56 * 2**20),
    )(*args)


def result_kernel(planes, slot_ref, *refs):
    far, core, middle, out_ref = refs[:planes], refs[planes], refs[planes + 1 : -1], refs[-1]
    images, real = out_ref.shape[0], out_ref.shape[2]
    _, _, per, width = far[0].shape
    count = middle[0].shape[0]
    for i in range(images):
        rows = [r[2 * y, i] for r in far for y in range(2)]
        rows = jnp.concatenate(rows + [core[:, i].reshape(2 * planes * per, width)], axis=0)
        table = slot_table(slot_ref, i, rows.shape[0], 4)
        out = middle[i // count][i % count] + dot(table, rows, 0, 0)
        out_ref[i, 0] = out.astype(BF)[0:real]


def result_call(far, core, slot, middle, shape):
    return pl.pallas_call(
        functools.partial(result_kernel, len(far)), out_shape=jax.ShapeDtypeStruct(shape, BF),
        cost_estimate=pl.CostEstimate(flops=3450000000, bytes_accessed=1, transcendentals=0),
        compiler_params=pltpu.CompilerParams(vmem_limit_bytes=32 * 2**20),
    )(slot, *far, core, *middle)


def flips(size, bit):
    return [(i, i ^ bit) for i in range(size)]


def in_order(parts, index):
    while len(parts) > 1:
        half = len(parts) // 2
        high = (index // half) % 2 == 1
        low, top = parts[:half], parts[half:]
        parts_low = [jnp.where(high, t, l) for l, t in zip(low, top)]
        parts_top = [jnp.where(high, l, t) for l, t in zip(low, top)]
        index = index % half
        if half == 1:
            return [parts_low[0], parts_top[0]]
        return in_order(parts_low, index) + in_order(parts_top, index)
    return parts


def hop(v, size, bit):
    return lax.ppermute(v, "fsdp", flips(size, bit))


def gather_far(piece, size):
    far = [piece] + [hop(piece, size, 4 * k) for k in range(1, size // 4)]
    return jnp.stack(in_order(far, lax.axis_index("fsdp") // 4))


def gather_near(held, size, bit):
    came = hop(held, size, bit)
    axis = 1 if bit == 2 else 2
    mine = (lax.axis_index("fsdp") // bit) % 2
    side = lax.broadcasted_iota(jnp.int32, held.shape[:axis] + (2,) + held.shape[axis:], axis)
    return jnp.where(side == mine, jnp.expand_dims(held, axis), jnp.expand_dims(came, axis))


def side_hop(far, size):
    return hop(jnp.stack([p[2:4] for p in far]), size, 2)


def core_hop(far, side, size):
    return hop(jnp.concatenate([p[1:2] for p in far] + [side[:, 1]]), size, 1)


def after(value, *others):
    return lax.optimization_barrier((value,) + others)[0]


def scatter_sum(keep, send, size, replicas, between, *wait):
    index = lax.axis_index("fsdp")
    planes = size // 4
    held = keep + hop(send, size, 1).astype(F32)
    rows = held.shape[0] // (planes * 2)
    held = held.reshape(planes, 2, rows, -1)
    high = (index // 2) % 2 == 1
    gone = jnp.where(high, held[:, 0], held[:, 1]).astype(BF)
    between[0](gone)
    came = hop(after(gone, *wait), size, 2)
    held = jnp.where(high, held[:, 1], held[:, 0]) + came.astype(F32)
    low = held.astype(BF)
    place = index // 4
    total = lax.dynamic_index_in_dim(held, place, 0, keepdims=False)
    gone = [lax.dynamic_index_in_dim(low, place ^ k, 0, keepdims=False) for k in range(1, planes)]
    between[1](gone[0])
    for k in range(1, planes):
        total = total + hop(gone[k - 1], size, 4 * k).astype(F32)
    if replicas == 2:
        low = total.astype(BF)
        between[2](low)
        return low.astype(F32) + lax.ppermute(low, "replica", [(0, 1), (1, 0)]).astype(F32)
    return lax.psum(total, "replica")


def solution(mesh):
    replicas = mesh.shape["replica"]
    size = mesh.shape["fsdp"]

    def body(tokens_in, picks_in, ranks_in, capacity, first_gain, first_shift, attend_weight,
             output_weight, second_gain, second_shift, router_weight, expert_up, expert_down, cotangent):
        micro, _, length, width = tokens_in.shape
        experts = capacity.shape[0]
        slots = experts * CAP
        tall = -(-length // 128) * 128
        share = attend_weight.shape[0]
        vecs = jnp.stack([first_gain, first_shift, second_gain, second_shift])
        vecs = jnp.pad(vecs, ((0, 0), (0, 128 - share)))
        packed = pl.pallas_call(
            pack_kernel, out_shape=jax.ShapeDtypeStruct((share, 4 * width + 128), BF),
            cost_estimate=pl.CostEstimate(flops=2300000000, bytes_accessed=1, transcendentals=0),
        scratch_shapes=[pltpu.VMEM((128, 128), F32)],
        )(attend_weight, output_weight, router_weight, vecs)
        far = gather_far(packed, size)

        place = lax.axis_index("fsdp").astype(jnp.int32).reshape(1)
        meta = jnp.concatenate([picks_in[:, 0].transpose(0, 2, 1), ranks_in], axis=1).astype(F32)
        meta = jnp.pad(meta, ((0, 0), (0, 5), (0, tall - length)), constant_values=1000.0)
        slot, *cot_out = route_call(place, meta, capacity.astype(F32)[:, None], cotangent, size)
        count = micro // CHUNKS
        chunks = range(CHUNKS)
        near = gather_near(after(far, slot), size, 2)
        planes = size // 4

        def along_z(pieces, *wait):
            ready = lax.optimization_barrier((*wait, *pieces))[len(wait) :]
            return [q if k == 0 else hop(q, size, 4 * k) for k, q in enumerate(ready)]

        cot_far = [along_z(cot_out[c * planes : (c + 1) * planes], near if c else far) for c in chunks[:1 if F7 else None]]
        full = gather_near(near, size, 1).reshape(size * share, -1)

        def exchange(r):
            return lax.all_to_all(r, "fsdp", split_axis=0, concat_axis=0, tiled=True)

        def swap(v):
            return lax.ppermute(v, "replica", [(0, 1), (1, 0)])

        rows_in, cot_rows, saved = [], [], []
        for c in chunks:
            sent, *kept = forward_call(c, count, tokens_in, full, slot, size, slots)
            saved.append(kept)
            rows_in.append(exchange(after(sent, *cot_far[c])))
            arrived = lax.optimization_barrier((sent, *cot_far[c]))[1:]
            side = side_hop(arrived, size)
            cot_rows.append((*arrived, side, core_hop(arrived, side, size)))
            if F7 and c + 1 < CHUNKS:
                cot_far.append(along_z(cot_out[(c + 1) * planes : (c + 2) * planes], *((sent,) if F7 == 1 else (cot_far[0][1 : 1 + F7]))))
        paired = replicas == 2
        other_x = [swap(x) for x in rows_in] if paired else [()] * CHUNKS

        acc = None
        row_grads, router_grads, cot_kept = [], [], []
        for c in chunks:
            ready = after(place, other_x[c - 1]) if c > 0 and F1 else place
            w0, w1, r, kept, ug, dg, og = expert_call(True, c, micro, ready, rows_in[c : c + 1], cot_rows[c], full,
                                                      expert_up, expert_down, experts, acc)
            acc = (ug, dg, w0, w1)
            row_grads.append(exchange(r))
            router_grads.append(og)
            cot_kept.append(kept)
        acc, (result_near, result_side) = acc[:2], acc[2:]
        result_side = hop(result_side, size, 2)
        other_g = [swap(g) for g in cot_kept] if paired else [()] * CHUNKS
        box = [acc]

        def other(first, span, *wait):
            if paired:
                box[0] = expert_call(False, 0, micro, after(place, *wait), other_x, other_g, full,
                                     expert_up, expert_down, experts, box[0], first, span)

        sums = None
        half = expert_up.shape[0] // 2
        for c in chunks:
            last = c == CHUNKS - 1
            final = (after(place, box[0][0]) if F9 else place, *router_grads) if last else None
            slots_in = slot
            if c == 0 and F2 > 0:
                slots_in = after(slot, other_g[0], *other_x[: F2])
            if c == 1 and F3 > 0:
                slots_in = after(slot, *other_g, *other_x)
            sums = backward_call(c, count, row_grads[c], slots_in, tokens_in, cotangent, full, saved[c], sums, final)
            if c == CHUNKS - 2:
                if F5 == 1:
                    result_side = after(result_side, sums[1])
                if True:
                    other(0, half, *((result_side, sums[1]) if F4 else (sums[1],)))
                if F5 == 2:
                    result_side = after(result_side, box[0][0])
        result_far = along_z([jnp.concatenate([result_near[k], result_side[k]]) for k in range(planes)])
        token_grad, keep, send = sums
        tail = []
        total = scatter_sum(keep, send, size, replicas,
                            (lambda gone: other(half, half, gone) if F8 == 0 else other(half, half, keep) if F8 == 3 else other(half, half) if F8 == 4 else None,
                             lambda gone: (tail.append(gone), other(half, half, gone) if F8 == 2 else None), tail.append))
        acc = box[0]
        if not paired:
            acc = lax.psum(tuple(acc), "replica")
        up_grad, down_grad = acc
        if F6:
            late = (tail[F6 - 1],) if F6 < 3 else (box[0][0],) if F6 == 4 else (box[0][0], tail[0])
            result_far = lax.optimization_barrier((*late, *result_far))[len(late) :]
        result_core = hop(jnp.stack([p.reshape((2, 2) + p.shape[1:])[:, 1] for p in result_far]), size, 1)
        out = result_call(result_far, result_core.reshape((-1,) + result_core.shape[2:]), after(slot, *tail),
                          [s[4] for s in saved], tokens_in.shape)

        w = 4 * width + experts
        return (out, token_grad, total[:, w], total[:, w + 1], total[:, : 3 * width], total[:, 3 * width : 4 * width],
                total[:, w + 2], total[:, w + 3], total[:, 4 * width : w], up_grad, down_grad)

    split = ("replica", "fsdp")
    in_specs = (P(None, split), P(None, split), P(None, split), P(), P("fsdp"), P("fsdp"), P("fsdp"), P("fsdp"),
                P("fsdp"), P("fsdp"), P("fsdp"), P("fsdp"), P("fsdp"), P(None, split))
    out_specs = (P(None, split), P(None, split)) + (P("fsdp"),) * 9
    return jax.shard_map(body, mesh=mesh, in_specs=in_specs, out_specs=out_specs, check_vma=False)
```

```python
import functools

import jax
import jax.numpy as jnp
from jax import lax
from jax.experimental import pallas as pl
from jax.experimental.pallas import tpu as pltpu
from jax.sharding import PartitionSpec as P

HEADS = 6
HEAD_DIM = 64
CAP = 16
EPSILON = 1e-06
BF = jnp.bfloat16
F32 = jnp.float32
CHUNKS = 2
G = 0
F1, F2, F3, F4, F5, F6, F7, F8, F9, F10 = 1, 0, 1, 0, 0, 3, 0, 0, 1, 0
TILE = 1536
BLOCK = 256


def dot(a, b, ca, cb):
    return lax.dot_general(a, b, (((ca,), (cb,)), ((), ())), preferred_element_type=F32)


def norm_parts(values):
    center = values - jnp.mean(values, axis=-1, keepdims=True)
    inv = lax.rsqrt(jnp.mean(center * center, axis=-1, keepdims=True) + EPSILON)
    return center * inv, inv


def norm_back(grad, hat, inv, gain):
    scaled = grad * gain
    return inv * (
        scaled
        - jnp.mean(scaled, axis=-1, keepdims=True)
        - hat * jnp.mean(scaled * hat, axis=-1, keepdims=True)
    )


BEND = 0.31
TAIL = (0.12367170304059982, 0.12373026460409164, 0.11044304817914963, 0.09964941442012787,
        0.007125736679881811, 0.1295062005519867, -0.12619934976100922, 0.03207298368215561)

def gelu_pair(v):
    a = 1.0 + BEND * jnp.abs(v)
    k = pl.reciprocal(a, approx=False)
    bell = jnp.exp(v * v * -0.5)
    p = TAIL[7]
    for c in TAIL[6::-1]:
        p = p * k + c
    half = p * k * bell
    phi = jnp.where(v >= 0, 1.0 - half, half)
    return v * phi, phi + v * bell * 0.3989422804014327

def expert_kernel(own, acc, experts, first, local, planes, place_ref, rt_ref, up_ref, down_ref, *rest):
    rest = list(rest)

    def take(n):
        got = rest[:n]
        del rest[:n]
        return got

    x_refs = take(1 if own else CHUNKS)
    g_refs = take(planes + 2 if own else CHUNKS)
    if acc:
        up_in, down_in = take(2)
    if own:
        w_refs = take(planes)
        rg_ref, cot_ref = take(2)
    ug_ref, dg_ref = take(2)
    if own:
        og_ref, = take(1)
        xt, back, cots, gates_s, hid, pg, prod, rowg = rest
    else:
        xt, back, cots, xs, hid, pg = rest
    e = pl.program_id(0); f = pl.program_id(1)
    nf = pl.num_programs(1)
    R = back.shape[0]
    width = back.shape[1]
    groups = 4 * planes
    def rows(refs):
        return jnp.concatenate([r[...].reshape(R // len(refs), width) for r in refs], axis=0)
    lane = lax.broadcasted_iota(jnp.int32, (1, 128), 1)
    mine = lane == place_ref[0] * local + first + e

    @pl.when(f == 0)
    def _():
        x = rows(x_refs)
        if not own:
            xs[...] = x
        logits = dot(x, rt_ref[...], 1, 0)
        logits = jnp.where(lane < experts, logits, -1e30)
        top = jnp.max(logits, axis=1, keepdims=True)
        raised = jnp.exp(logits - top)
        gates = raised / jnp.sum(raised, axis=1, keepdims=True)
        gate = jnp.sum(jnp.where(mine, gates, 0.0), axis=1, keepdims=True)
        if own:
            per = R // groups
            side, core = g_refs[planes:]
            for k in range(planes):
                for j, got in ((0, g_refs[k][0]), (2, side[k, 0]), (1, core[k]), (3, core[planes + k])):
                    at = pl.multiple_of(((4 * k + j) ^ place_ref[0]) * per, per)
                    cots[pl.ds(at, per), :] = got.reshape(per, width)
            cot_ref[...] = cots[...].reshape(cot_ref.shape)
        else:
            cots[...] = rows(g_refs)
        back[...] = (gate * cots[...].astype(F32)).astype(BF)
        xt[...] = x.T
        if own:
            gates_s[...] = gates

    x = rows(x_refs) if own else xs[...]
    step = min(BLOCK, R)
    for b in range(R // step):
        sl = slice(b * step, (b + 1) * step)
        h, d = gelu_pair(dot(x[sl], up_ref[0], 1, 0))
        hid[sl, :] = h.astype(BF)
        pg[sl, :] = (d * dot(back[sl, :], down_ref[0], 1, 1)).astype(BF)
    ug = dot(xt[...], pg[...], 1, 0)
    dg = dot(hid[...], back[...], 0, 0)
    if acc:
        ug = ug + up_in[0]; dg = dg + down_in[0]
    ug_ref[0] = ug
    dg_ref[0] = dg
    if own:
        p = dot(hid[...], down_ref[0], 1, 0)
        r = dot(pg[...], up_ref[0], 1, 1)
        @pl.when(f == 0)
        def _():
            prod[...] = p
            rowg[...] = r
        @pl.when(f > 0)
        def _():
            prod[...] += p
            rowg[...] += r
        @pl.when(f == nf - 1)
        def _():
            gates = gates_s[...]
            gate = jnp.sum(jnp.where(mine, gates, 0.0), axis=1, keepdims=True)
            back[...] = (gate * prod[...]).astype(BF)
            per = R // groups
            for j in range(groups):
                got = back[pl.ds(pl.multiple_of((j ^ place_ref[0]) * per, per), per), :]
                w_refs[j // 4][j % 4] = got.reshape(w_refs[0].shape[1:])
            gg = jnp.sum(cots[...].astype(F32) * prod[...], axis=1, keepdims=True)
            lg = (gates * (jnp.where(mine, gg, 0.0) - gate * gg)).astype(BF)
            rg_ref[...] = (rowg[...] + dot(lg, rt_ref[...], 1, 1)).astype(BF).reshape(rg_ref.shape)
            og = dot(xt[...], lg, 1, 0)
            @pl.when(e == 0)
            def _():
                og_ref[...] = og
            @pl.when(e > 0)
            def _():
                og_ref[...] += og

def expert_call(own, place, xs, gs, full, up, down, experts, acc=None, first=0, span=None, tile=TILE):
    groups, imgs, lc, width = xs[0].shape
    local, _, ff = up.shape
    cap = lc // local
    planes = groups // 4
    R = groups * imgs * cap * len(xs)
    span = local if span is None else span
    block = pl.BlockSpec((groups, imgs, cap, width), lambda e, f: (0, 0, e + first, 0))
    upb = pl.BlockSpec((1, width, tile), lambda e, f: (e + first, 0, f))
    dnb = pl.BlockSpec((1, tile, width), lambda e, f: (e + first, f, 0))
    last = full.shape[1] // 128 - 1
    in_specs = [pl.BlockSpec(memory_space=pltpu.SMEM), pl.BlockSpec((width, 128), lambda e, f: (0, last)), upb, dnb]
    in_specs += [block] * len(xs)
    if own:
        in_specs += [pl.BlockSpec((1, imgs, cap, width), lambda e, f: (0, 0, e, 0))] * planes
        in_specs += [pl.BlockSpec((planes, 1, imgs, cap, width), lambda e, f: (0, 0, 0, e, 0)),
                     pl.BlockSpec((2 * planes, imgs, cap, width), lambda e, f: (0, 0, e, 0))]
    else:
        in_specs += [block] * len(gs)
    args = [place, full, up, down, *xs, *gs]
    out_shape, out_specs, alias = [], [], {}
    if own:
        out_shape += [jax.ShapeDtypeStruct((4, imgs, lc, width), BF)] * planes
        out_shape += [jax.ShapeDtypeStruct(xs[0].shape, BF)] * 2
        out_specs += [pl.BlockSpec((4, imgs, cap, width), lambda e, f: (0, 0, e, 0))] * planes + [block] * 2
    if acc is not None:
        at = len(args)
        alias = {at: len(out_shape), at + 1: len(out_shape) + 1}
        in_specs += [upb, dnb]
        args += list(acc)
    out_shape += [jax.ShapeDtypeStruct(up.shape, F32), jax.ShapeDtypeStruct(down.shape, F32)]
    out_specs += [upb, dnb]
    scratch = [pltpu.VMEM((width, R), BF), pltpu.VMEM((R, width), BF), pltpu.VMEM((R, width), BF)]
    if own:
        out_shape.append(jax.ShapeDtypeStruct((width, 128), F32))
        out_specs.append(pl.BlockSpec((width, 128), lambda e, f: (0, 0)))
        scratch.append(pltpu.VMEM((R, 128), F32))
    else:
        scratch.append(pltpu.VMEM((R, width), BF))
    scratch += [pltpu.VMEM((R, tile), BF), pltpu.VMEM((R, tile), BF)]
    if own:
        scratch += [pltpu.VMEM((R, width), F32)] * 2
    return pl.pallas_call(
        functools.partial(expert_kernel, own, acc is not None, experts, first, local, planes),
        grid=(span, ff // tile), in_specs=in_specs, out_specs=out_specs, out_shape=out_shape,
        scratch_shapes=scratch, input_output_aliases=alias,
        cost_estimate=pl.CostEstimate(flops=int((20 * 1.5 if own else 15 * 0.7 * span) * 1.15e9), bytes_accessed=1, transcendentals=0),
        compiler_params=pltpu.CompilerParams(vmem_limit_bytes=56 * 2**20, dimension_semantics=("arbitrary", "arbitrary")),
    )(*args)


def vec_rows(pack_ref, at):
    return pack_ref[:, at:].astype(F32).T


def slot_table(slot_ref, i, slots, at=0):
    rows = lax.broadcasted_iota(jnp.int32, (slots, slot_ref.shape[2]), 0)
    return ((rows == slot_ref[i, at : at + 1, :]) | (rows == slot_ref[i, at + 1 : at + 2, :])).astype(F32).astype(BF)


def route_kernel(experts, place_ref, meta_ref, cap_ref, cot_ref, slot_ref, *rest):
    rows_refs, wide = rest[:-1], rest[-1]
    groups = 4 * len(rows_refs) // CHUNKS
    per = experts * CAP // groups
    images, _, length = meta_ref.shape
    limit_of = cap_ref[...]
    wide[...] = jnp.zeros_like(wide)
    real = cot_ref.shape[2]
    for i in range(images):
        meta = meta_ref[i]
        order = meta[2:3, :]
        earlier = (meta.T[:, 2:3] < order).astype(F32).astype(BF)
        labels = lax.broadcasted_iota(jnp.int32, (experts, length), 0).astype(F32)
        hits = [labels == meta[c : c + 1, :] for c in range(2)]
        ones = [h.astype(F32) for h in hits]
        before = [dot(ones[0].astype(BF), earlier, 1, 0)]
        before.append(dot(ones[1].astype(BF), earlier, 1, 0) + jnp.sum(ones[0], axis=1, keepdims=True))
        for c in range(2):
            position = jnp.sum(ones[c] * before[c], axis=0, keepdims=True)
            limit = jnp.sum(ones[c] * limit_of, axis=0, keepdims=True)
            slot = jnp.where(position < limit, meta[c : c + 1, :] * CAP + position, -1.0)
            slot = slot.astype(jnp.int32)
            slot_ref[i, c : c + 1, :] = slot
            near = slot ^ (place_ref[0] * per)
            slot_ref[i, 2 + c : 3 + c, :] = jnp.where(slot >= 0, near, -1)
        slot_ref[i, 4:, :] = jnp.full((4, length), -1, jnp.int32)
        wide[i, 0:real, :] = cot_ref[i, 0].astype(F32)
        rows = dot(slot_table(slot_ref, i, experts * CAP, 2), wide[i].astype(BF), 1, 0).astype(BF)
        planes = groups // 4
        count = rows_refs[0].shape[1]
        rows = rows.reshape(planes, 4, per, rows.shape[1])
        for k in range(planes):
            rows_refs[i // count * planes + k][:, i % count] = rows[k]


def route_call(place, meta, limits, cot, size):
    images, _, length = meta.shape
    experts = limits.shape[0]
    width = cot.shape[-1]
    vmem = pl.BlockSpec(memory_space=pltpu.VMEM)
    planes = size // 4
    return pl.pallas_call(
        functools.partial(route_kernel, experts),
        in_specs=[pl.BlockSpec(memory_space=pltpu.SMEM), vmem, vmem, vmem],
        out_shape=[jax.ShapeDtypeStruct((images, 8, length), jnp.int32)]
        + [jax.ShapeDtypeStruct((4, images // CHUNKS, experts * CAP // size, width), BF)] * (planes * CHUNKS),
        scratch_shapes=[pltpu.VMEM((images, length, width), F32)],
        cost_estimate=pl.CostEstimate(flops=3450000000, bytes_accessed=1, transcendentals=0),
        compiler_params=pltpu.CompilerParams(vmem_limit_bytes=48 * 2**20),
    )(place, meta, limits, cot)


def pack_kernel(attend_ref, output_ref, router_ref, vec_ref, out_ref, tall):
    rows, wide = attend_ref.shape
    width = output_ref.shape[1]
    out_ref[:, :wide] = attend_ref[...]
    out_ref[:, wide : wide + width] = output_ref[...]
    tall[...] = jnp.zeros_like(tall)
    experts = router_ref.shape[1]
    tall[0:rows, 0:experts] = router_ref[...].astype(F32)
    vecs = jnp.concatenate([vec_ref[...].astype(F32), jnp.zeros((4, 128), F32)], axis=0)
    turned = jnp.concatenate([vecs] + [jnp.zeros((120, 128), F32)], axis=0).T
    lane = lax.broadcasted_iota(jnp.int32, (128, 128), 1)
    full = jnp.where(lane < experts, tall[...], jnp.roll(turned, experts, axis=1))
    out_ref[:, wide + width :] = full[0:rows].astype(BF)


def half_masks(width):
    lane = lax.broadcasted_iota(jnp.int32, (1, width), 1)
    return [(lane < HEAD_DIM).astype(F32).astype(BF), (lane >= HEAD_DIM).astype(F32).astype(BF)]


def forward_kernel(tok_ref, pack_ref, slot_ref, rows_ref, normed_ref, joined_ref, probs_ref, mixed_ref,
                   middle_ref, wide, heads):
    images, _, real, width = tok_ref.shape
    length = slot_ref.shape[2]
    groups, _, per, _ = rows_ref.shape
    experts = groups * per // CAP
    vecs = vec_rows(pack_ref, 4 * width)[experts : experts + 4]
    gain_one, shift_one, gain_two, shift_two = (vecs[k : k + 1] for k in range(4))
    masks = half_masks(2 * HEAD_DIM)
    key_real = lax.broadcasted_iota(jnp.int32, (1, length), 1) < real
    wide[...] = jnp.zeros_like(wide)
    for i in range(images):
        wide[i, 0:real, :] = tok_ref[i, 0].astype(F32)
        tokens = wide[i]
        hat, _ = norm_parts(tokens)
        normed = (hat * gain_one + shift_one).astype(BF)
        normed_ref[i] = normed
        joined = dot(normed, pack_ref[:, : 3 * width], 1, 0).astype(BF)
        joined_ref[i] = joined
        for pair in range(HEADS // 2):
            at = pair * 2 * HEAD_DIM
            q = joined[:, at : at + 2 * HEAD_DIM] * jnp.asarray(HEAD_DIM ** (-0.5), BF)
            k = joined[:, width + at : width + at + 2 * HEAD_DIM]
            v = joined[:, 2 * width + at : 2 * width + at + 2 * HEAD_DIM]
            both = None
            for s in range(2):
                scores = dot(q * masks[s], k, 1, 1)
                scores = jnp.where(key_real, scores, -1e30)
                raised = jnp.exp(scores - jnp.max(scores, axis=1, keepdims=True))
                probs = raised / jnp.sum(raised, axis=1, keepdims=True)
                probs = probs.astype(BF)
                probs_ref[i, 2 * pair + s] = probs
                got = dot(probs, v * masks[s], 1, 0)
                both = got if both is None else both + got
            heads[i, :, at : at + 2 * HEAD_DIM] = both.astype(BF)
        mixed = heads[i]
        mixed_ref[i] = mixed
        middle = tokens + dot(mixed, pack_ref[:, 3 * width : 4 * width], 1, 0)
        middle_ref[i] = middle
        hat_two, _ = norm_parts(middle)
        second = (hat_two * gain_two + shift_two).astype(BF)
        rows = dot(slot_table(slot_ref, i, groups * per), second, 1, 0)
        rows_ref[:, i] = rows.astype(BF).reshape(groups, per, width)


def whole(shape):
    return pl.BlockSpec(shape, lambda _: (0,) * len(shape))


def part_of(shape, count, chunk):
    return pl.BlockSpec((count,) + tuple(shape[1:]), lambda _: (chunk,) + (0,) * (len(shape) - 1))


def forward_call(chunk, count, tokens_in, pack, slot, size, slots):
    width = tokens_in.shape[-1]
    length = slot.shape[2]
    shapes = [((size, count, slots // size, width), BF), ((count, length, width), BF), ((count, length, 3 * width), BF),
              ((count, HEADS, length, length), BF), ((count, length, width), BF), ((count, length, width), F32)]
    return pl.pallas_call(
        forward_kernel, grid=(1,),
        in_specs=[part_of(tokens_in.shape, count, chunk), whole(pack.shape),
                  part_of(slot.shape, count, chunk)],
        out_specs=[whole(s) for s, _ in shapes],
        out_shape=[jax.ShapeDtypeStruct(s, d) for s, d in shapes],
        scratch_shapes=[pltpu.VMEM((count, length, width), F32), pltpu.VMEM((count, length, width), BF)],
        cost_estimate=pl.CostEstimate(flops=6440000000, bytes_accessed=1, transcendentals=0),
        compiler_params=pltpu.CompilerParams(vmem_limit_bytes=56 * 2**20),
    )(tokens_in, pack, slot)


def backward_kernel(chunk, acc, last, *refs):
    refs = list(refs)
    (rows_ref, slot_ref, tok_ref, cot_ref, pack_ref, normed_ref, joined_ref, probs_ref, mixed_ref,
     middle_ref) = refs[:10]
    refs = refs[10:]
    if acc:
        attend_in, output_in, vec_in = refs[:3]
        refs = refs[4:]
    if last:
        place_ref, router_in = refs[0], refs[1 : 1 + CHUNKS]
        refs = refs[1 + CHUNKS :]
        grad_ref, keep_ref, send_ref, wide, joined_grad, tall = refs
    else:
        grad_ref, attend_ref, output_ref, vec_ref, wide, joined_grad, tall = refs
    images, _, real, width = tok_ref.shape
    length = slot_ref.shape[2]
    groups, _, per, _ = rows_ref.shape
    experts = groups * per // CAP
    vecs = vec_rows(pack_ref, 4 * width)[experts : experts + 4]
    gain_one, _, gain_two, _ = (vecs[k : k + 1] for k in range(4))
    masks = half_masks(2 * HEAD_DIM)
    scale = HEAD_DIM ** (-0.5)
    attend_sum = output_sum = None
    sums = [None] * 4
    def add(old, new):
        return new if old is None else old + new
    wide[...] = jnp.zeros_like(wide)
    for i in range(images):
        wide[0, i, 0:real, :] = tok_ref[i, 0].astype(F32)
        wide[1, i, 0:real, :] = cot_ref[i, 0].astype(F32)
        table = slot_table(slot_ref, i, groups * per)
        second_grad = dot(table, rows_ref[:, i].reshape(groups * per, width), 0, 0)
        middle = middle_ref[i]
        hat_two, inv_two = norm_parts(middle)
        sums[2] = add(sums[2], jnp.sum(second_grad * hat_two, axis=0, keepdims=True))
        sums[3] = add(sums[3], jnp.sum(second_grad, axis=0, keepdims=True))
        middle_grad = wide[1, i] + norm_back(second_grad, hat_two, inv_two, gain_two)
        branch_grad = middle_grad.astype(BF)
        output_sum = add(output_sum, dot(mixed_ref[i], branch_grad, 0, 0))
        mixed_grad = dot(branch_grad, pack_ref[:, 3 * width : 4 * width], 1, 1).astype(BF)
        joined = joined_ref[i]
        for pair in range(HEADS // 2):
            at = pair * 2 * HEAD_DIM
            q = joined[:, at : at + 2 * HEAD_DIM]
            k = joined[:, width + at : width + at + 2 * HEAD_DIM]
            v = joined[:, 2 * width + at : 2 * width + at + 2 * HEAD_DIM]
            m = mixed_grad[:, at : at + 2 * HEAD_DIM]
            vg = qg = kg = None
            for s in range(2):
                low = probs_ref[i, 2 * pair + s]
                ms = m * masks[s]
                vg = add(vg, dot(low, ms, 0, 0))
                probs = low.astype(F32)
                probs_grad = dot(ms, v, 1, 1)
                weighed = probs * probs_grad
                scores_grad = (weighed - probs * jnp.sum(weighed, axis=1, keepdims=True)).astype(BF)
                qg = add(qg, dot(scores_grad, k * masks[s], 1, 0))
                kg = add(kg, dot(scores_grad, q * masks[s], 0, 0))
            joined_grad[i, :, at : at + 2 * HEAD_DIM] = (qg * scale).astype(BF)
            joined_grad[i, :, width + at : width + at + 2 * HEAD_DIM] = (kg * scale).astype(BF)
            joined_grad[i, :, 2 * width + at : 2 * width + at + 2 * HEAD_DIM] = vg.astype(BF)
        grads = joined_grad[i]
        attend_sum = add(attend_sum, dot(normed_ref[i], grads, 0, 0))
        normed_grad = dot(grads, pack_ref[:, : 3 * width], 1, 1)
        hat_one, inv_one = norm_parts(wide[0, i])
        sums[0] = add(sums[0], jnp.sum(normed_grad * hat_one, axis=0, keepdims=True))
        sums[1] = add(sums[1], jnp.sum(normed_grad, axis=0, keepdims=True))
        total = (middle_grad + norm_back(normed_grad, hat_one, inv_one, gain_one)).astype(BF)
        grad_ref[i, 0] = total[0:real]
    tall[...] = jnp.zeros_like(tall)
    for k in range(4):
        tall[experts + k : experts + k + 1, :] = sums[k]
    if acc:
        attend_sum = attend_sum + attend_in[...]
        output_sum = output_sum + output_in[...]
    vec = tall[...].T
    if acc:
        vec = vec + vec_in[...]
    if not last:
        attend_ref[...] = attend_sum
        output_ref[...] = output_sum
        vec_ref[...] = vec
        return
    odd = place_ref[0] % 2 == 1
    for part in router_in:
        vec = vec + part[...]
    for value, start in ((attend_sum, 0), (output_sum, 3 * width), (vec, 4 * width)):
        halves = value.reshape(groups // 2, 2, width // groups, value.shape[1])
        zero, one = (halves[:, k].reshape(width // 2, value.shape[1]) for k in range(2))
        at = slice(start, start + value.shape[1])
        keep_ref[:, at] = jnp.where(odd, one, zero)
        send_ref[:, at] = jnp.where(odd, zero, one).astype(BF)


def backward_call(chunk, count, rows, slot, tokens_in, cot, pack, saved, acc, final):
    width = tokens_in.shape[-1]
    length = slot.shape[2]
    args = [rows, slot, tokens_in, cot, pack] + list(saved)
    specs = [whole(rows.shape), part_of(slot.shape, count, chunk), part_of(tokens_in.shape, count, chunk),
             part_of(cot.shape, count, chunk), whole(pack.shape)] + [whole(s.shape) for s in saved]
    sums = [(width, 3 * width), (width, width), (width, 128)]
    alias = {}
    if acc is not None:
        args += list(acc[1:]) + [acc[0]]
        specs += [whole(s) for s in sums] + [pl.BlockSpec(memory_space=pl.ANY)]
        alias = {len(args) - 1: 0}
    kinds = [(s, F32) for s in sums]
    if final is not None:
        args += list(final)
        specs += [pl.BlockSpec(memory_space=pltpu.SMEM)] + [whole(v.shape) for v in final[1:]]
        kinds = [((width // 2, 4 * width + 128), d) for d in (F32, BF)]
    return pl.pallas_call(
        functools.partial(backward_kernel, chunk, acc is not None, final is not None), grid=(1,),
        in_specs=specs, out_specs=[part_of(tokens_in.shape, count, chunk)] + [whole(s) for s, _ in kinds],
        out_shape=[jax.ShapeDtypeStruct(tokens_in.shape, BF)] + [jax.ShapeDtypeStruct(s, d) for s, d in kinds],
        scratch_shapes=[pltpu.VMEM((2, count, length, width), F32), pltpu.VMEM((count, length, 3 * width), BF),
                        pltpu.VMEM((128, width), F32)],
        input_output_aliases=alias,
        cost_estimate=pl.CostEstimate(flops=8855000000, bytes_accessed=1, transcendentals=0),
        compiler_params=pltpu.CompilerParams(vmem_limit_bytes=56 * 2**20),
    )(*args)


def result_kernel(planes, slot_ref, side, core, *refs):
    far, middle, out_ref = refs[: planes * CHUNKS], refs[planes * CHUNKS : -1], refs[-1]
    images, real = out_ref.shape[0], out_ref.shape[2]
    count = middle[0].shape[0]
    for i in range(images):
        c, at = i // count, i % count
        rows = []
        for n in range(c * planes, (c + 1) * planes):
            rows += [far[n][0, at], core[n, at], side[n, 0, at], core[planes * CHUNKS + n, at]]
        rows = jnp.concatenate(rows, axis=0)
        table = slot_table(slot_ref, i, rows.shape[0], 2)
        out_ref[i, 0] = (middle[c][at] + dot(table, rows, 0, 0)).astype(BF)[0:real]


def result_call(far, side, core, slot, middle, shape):
    return pl.pallas_call(
        functools.partial(result_kernel, len(far) // CHUNKS), out_shape=jax.ShapeDtypeStruct(shape, BF),
        cost_estimate=pl.CostEstimate(flops=3450000000, bytes_accessed=1, transcendentals=0),
        compiler_params=pltpu.CompilerParams(vmem_limit_bytes=32 * 2**20),
    )(slot, side, core, *far, *middle)


def flips(size, bit):
    return [(i, i ^ bit) for i in range(size)]


def in_order(parts, index):
    while len(parts) > 1:
        half = len(parts) // 2
        high = (index // half) % 2 == 1
        low, top = parts[:half], parts[half:]
        parts_low = [jnp.where(high, t, l) for l, t in zip(low, top)]
        parts_top = [jnp.where(high, l, t) for l, t in zip(low, top)]
        index = index % half
        if half == 1:
            return [parts_low[0], parts_top[0]]
        return in_order(parts_low, index) + in_order(parts_top, index)
    return parts


def hop(v, size, bit):
    return lax.ppermute(v, "fsdp", flips(size, bit))


def gather_far(piece, size):
    far = [piece] + [hop(piece, size, 4 * k) for k in range(1, size // 4)]
    return jnp.stack(in_order(far, lax.axis_index("fsdp") // 4))


def gather_near(held, size, bit):
    came = hop(held, size, bit)
    axis = 1 if bit == 2 else 2
    mine = (lax.axis_index("fsdp") // bit) % 2
    side = lax.broadcasted_iota(jnp.int32, held.shape[:axis] + (2,) + held.shape[axis:], axis)
    return jnp.where(side == mine, jnp.expand_dims(held, axis), jnp.expand_dims(came, axis))


def side_hop(far, size):
    return hop(jnp.stack([p[2:4] for p in far]), size, 2)


def core_hop(far, side, size):
    return hop(jnp.concatenate([p[1:2] for p in far] + [side[:, 1]]), size, 1)


def after(value, *others):
    return lax.optimization_barrier((value,) + others)[0]


def scatter_sum(keep, send, size, replicas, between, *wait):
    index = lax.axis_index("fsdp")
    planes = size // 4
    held = keep + hop(send, size, 1).astype(F32)
    rows = held.shape[0] // (planes * 2)
    held = held.reshape(planes, 2, rows, -1)
    high = (index // 2) % 2 == 1
    gone = jnp.where(high, held[:, 0], held[:, 1]).astype(BF)
    between[0](gone)
    came = hop(after(gone, *wait), size, 2)
    held = jnp.where(high, held[:, 1], held[:, 0]) + came.astype(F32)
    low = held.astype(BF)
    place = index // 4
    total = lax.dynamic_index_in_dim(held, place, 0, keepdims=False)
    gone = [lax.dynamic_index_in_dim(low, place ^ k, 0, keepdims=False) for k in range(1, planes)]
    between[1](gone[0])
    for k in range(1, planes):
        total = total + hop(gone[k - 1], size, 4 * k).astype(F32)
    if replicas == 2:
        low = total.astype(BF)
        between[2](low)
        return low.astype(F32) + lax.ppermute(low, "replica", [(0, 1), (1, 0)]).astype(F32)
    return lax.psum(total, "replica")


def solution(mesh):
    replicas = mesh.shape["replica"]
    size = mesh.shape["fsdp"]

    def body(tokens_in, picks_in, ranks_in, capacity, first_gain, first_shift, attend_weight,
             output_weight, second_gain, second_shift, router_weight, expert_up, expert_down, cotangent):
        micro, _, length, width = tokens_in.shape
        experts = capacity.shape[0]
        slots = experts * CAP
        tall = -(-length // 128) * 128
        share = attend_weight.shape[0]
        vecs = jnp.stack([first_gain, first_shift, second_gain, second_shift])
        vecs = jnp.pad(vecs, ((0, 0), (0, 128 - share)))
        packed = pl.pallas_call(
            pack_kernel, out_shape=jax.ShapeDtypeStruct((share, 4 * width + 128), BF),
            cost_estimate=pl.CostEstimate(flops=2300000000, bytes_accessed=1, transcendentals=0),
        scratch_shapes=[pltpu.VMEM((128, 128), F32)],
        )(attend_weight, output_weight, router_weight, vecs)
        far = gather_far(packed, size)

        place = lax.axis_index("fsdp").astype(jnp.int32).reshape(1)
        meta = jnp.concatenate([picks_in[:, 0].transpose(0, 2, 1), ranks_in], axis=1).astype(F32)
        meta = jnp.pad(meta, ((0, 0), (0, 5), (0, tall - length)), constant_values=1000.0)
        slot, *cot_out = route_call(place, meta, capacity.astype(F32)[:, None], cotangent, size)
        count = micro // CHUNKS
        chunks = range(CHUNKS)
        near = gather_near(after(far, slot), size, 2)
        planes = size // 4

        def along_z(pieces, *wait):
            ready = lax.optimization_barrier((*wait, *pieces))[len(wait) :]
            return [q if k == 0 else hop(q, size, 4 * k) for k, q in enumerate(ready)]

        cot_far = [along_z(cot_out[c * planes : (c + 1) * planes], near if c else far) for c in chunks[:1 if F7 else None]]
        full = gather_near(near, size, 1).reshape(size * share, -1)

        def exchange(r):
            return lax.all_to_all(r, "fsdp", split_axis=0, concat_axis=0, tiled=True)

        def swap(v):
            return lax.ppermute(v, "replica", [(0, 1), (1, 0)])

        rows_in, cot_rows, saved = [], [], []
        for c in chunks:
            sent, *kept = forward_call(c, count, tokens_in, full, slot, size, slots)
            saved.append(kept)
            rows_in.append(exchange(after(sent, *cot_far[c])))
            arrived = lax.optimization_barrier((sent, *cot_far[c]))[1:]
            side = side_hop(arrived, size)
            cot_rows.append((*arrived, side, core_hop(arrived, side, size)))
            if F7 and c + 1 < CHUNKS:
                cot_far.append(along_z(cot_out[(c + 1) * planes : (c + 2) * planes], *((sent,) if F7 == 1 else (cot_far[0][1 : 1 + F7]))))
        paired = replicas == 2
        other_x = [swap(x) for x in rows_in] if paired else [()] * CHUNKS

        acc = None
        row_grads, router_grads, cot_kept, result_far = [], [], [], []
        for c in chunks:
            ready = after(place, other_x[c - 1]) if c > 0 and F1 else place
            *w, r, kept, ug, dg, og = expert_call(True, ready, rows_in[c : c + 1], cot_rows[c], full,
                                                  expert_up, expert_down, experts, acc)
            acc = (ug, dg)
            row_grads.append(exchange(r))
            router_grads.append(og)
            cot_kept.append(kept)
            result_far.append(along_z(w))
        other_g = [swap(g) for g in cot_kept] if paired else [()] * CHUNKS
        box = [acc]

        def other(first, span, *wait):
            if paired:
                box[0] = expert_call(False, after(place, *wait), other_x, other_g, full,
                                     expert_up, expert_down, experts, box[0], first, span)

        sums = None
        half = expert_up.shape[0] // 2
        for c in chunks:
            last = c == CHUNKS - 1
            final = (after(place, box[0][0]) if F9 else place, *router_grads) if last else None
            slots_in = slot
            if c == 0 and F2 > 0:
                slots_in = after(slot, other_g[0], *other_x[: F2])
            if c == 1 and F3 > 0:
                slots_in = after(slot, *other_g, *other_x)
            if (F4, F5)[c] > 0:
                slots_in = after(slots_in, *result_far[c][1 : 1 + (F4, F5)[c]])
            sums = backward_call(c, count, row_grads[c], slots_in, tokens_in, cotangent, full, saved[c], sums, final)
            if c == CHUNKS - 2:
                other(0, half, sums[1])
                early = box[0][0]
                if F8 == 5:
                    other(half, half)
        token_grad, keep, send = sums
        every = [p for far in result_far for p in far]
        if F7 != 9:
            every = list(lax.optimization_barrier((early if G else keep, *every))[1:])
        side = side_hop(every, size)
        tail = []
        total = scatter_sum(keep, send, size, replicas,
                            (lambda gone: other(half, half, gone) if F8 == 0 else None,
                             lambda gone: (tail.append(gone), other(half, half, gone) if F8 == 2 else None), tail.append),
                            *((side,) if F10 else ()))
        acc = box[0]
        if not paired:
            acc = lax.psum(tuple(acc), "replica")
        up_grad, down_grad = acc
        side_in = side
        if F6:
            late = (tail[F6 - 1],) if F6 < 3 else (box[0][0],) if F6 == 4 else (box[0][0], tail[0])
            side_in = after(side, *late)
        out = result_call(every, side, core_hop(every, side_in, size), after(slot, *tail), [s[4] for s in saved], tokens_in.shape)

        w = 4 * width + experts
        return (out, token_grad, total[:, w], total[:, w + 1], total[:, : 3 * width], total[:, 3 * width : 4 * width],
                total[:, w + 2], total[:, w + 3], total[:, 4 * width : w], up_grad, down_grad)

    split = ("replica", "fsdp")
    in_specs = (P(None, split), P(None, split), P(None, split), P(), P("fsdp"), P("fsdp"), P("fsdp"), P("fsdp"),
                P("fsdp"), P("fsdp"), P("fsdp"), P("fsdp"), P("fsdp"), P(None, split))
    out_specs = (P(None, split), P(None, split)) + (P("fsdp"),) * 9
    return jax.shard_map(body, mesh=mesh, in_specs=in_specs, out_specs=out_specs, check_vma=False)
```

```python
import functools

import jax
import jax.numpy as jnp
from jax import lax
from jax.experimental import pallas as pl
from jax.experimental.pallas import tpu as pltpu
from jax.sharding import PartitionSpec as P

HEADS = 6
HEAD_DIM = 64
CAP = 16
EPSILON = 1e-06
BF = jnp.bfloat16
F32 = jnp.float32
CHUNKS = 2
G = 0
F1, F2, F3, F4, F5, F6, F7, F8, F9, F10 = 1, 0, 1, 0, 0, 3, 0, 0, 1, 0
TILE = 1536
BLOCK = 256


def dot(a, b, ca, cb):
    return lax.dot_general(a, b, (((ca,), (cb,)), ((), ())), preferred_element_type=F32)


def norm_parts(values):
    center = values - jnp.mean(values, axis=-1, keepdims=True)
    inv = lax.rsqrt(jnp.mean(center * center, axis=-1, keepdims=True) + EPSILON)
    return center * inv, inv


def norm_back(grad, hat, inv, gain):
    scaled = grad * gain
    return inv * (
        scaled
        - jnp.mean(scaled, axis=-1, keepdims=True)
        - hat * jnp.mean(scaled * hat, axis=-1, keepdims=True)
    )


BEND = 0.31
TAIL = (0.12367170304059982, 0.12373026460409164, 0.11044304817914963, 0.09964941442012787,
        0.007125736679881811, 0.1295062005519867, -0.12619934976100922, 0.03207298368215561)

def gelu_pair(v):
    a = 1.0 + BEND * jnp.abs(v)
    k = pl.reciprocal(a, approx=False)
    bell = jnp.exp(v * v * -0.5)
    p = TAIL[7]
    for c in TAIL[6::-1]:
        p = p * k + c
    half = p * k * bell
    phi = jnp.where(v >= 0, 1.0 - half, half)
    return v * phi, phi + v * bell * 0.3989422804014327

def expert_kernel(own, acc, experts, first, local, planes, place_ref, rt_ref, up_ref, down_ref, *rest):
    rest = list(rest)

    def take(n):
        got = rest[:n]
        del rest[:n]
        return got

    x_refs = take(1 if own else CHUNKS)
    g_refs = take(planes + 2 if own else CHUNKS)
    if acc:
        up_in, down_in = take(2)
    if own:
        w_refs = take(planes)
        rg_ref, cot_ref = take(2)
    ug_ref, dg_ref = take(2)
    if own:
        og_ref, = take(1)
        xt, back, cots, gates_s, hid, pg, prod, rowg = rest
    else:
        xt, back, cots, xs, hid, pg = rest
    e = pl.program_id(0); f = pl.program_id(1)
    nf = pl.num_programs(1)
    R = back.shape[0]
    width = back.shape[1]
    groups = 4 * planes
    def rows(refs):
        return jnp.concatenate([r[...].reshape(R // len(refs), width) for r in refs], axis=0)
    lane = lax.broadcasted_iota(jnp.int32, (1, 128), 1)
    mine = lane == place_ref[0] * local + first + e

    @pl.when(f == 0)
    def _():
        x = rows(x_refs)
        if not own:
            xs[...] = x
        logits = dot(x, rt_ref[...], 1, 0)
        logits = jnp.where(lane < experts, logits, -1e30)
        top = jnp.max(logits, axis=1, keepdims=True)
        raised = jnp.exp(logits - top)
        gates = raised / jnp.sum(raised, axis=1, keepdims=True)
        gate = jnp.sum(jnp.where(mine, gates, 0.0), axis=1, keepdims=True)
        if own:
            per = R // groups
            side, core = g_refs[planes:]
            for k in range(planes):
                for j, got in ((0, g_refs[k][0]), (2, side[k, 0]), (1, core[k]), (3, core[planes + k])):
                    at = pl.multiple_of(((4 * k + j) ^ place_ref[0]) * per, per)
                    cots[pl.ds(at, per), :] = got.reshape(per, width)
            cot_ref[...] = cots[...].reshape(cot_ref.shape)
        else:
            cots[...] = rows(g_refs)
        back[...] = (gate * cots[...].astype(F32)).astype(BF)
        xt[...] = x.T
        if own:
            gates_s[...] = gates

    x = rows(x_refs) if own else xs[...]
    step = min(BLOCK, R)
    for b in range(R // step):
        sl = slice(b * step, (b + 1) * step)
        h, d = gelu_pair(dot(x[sl], up_ref[0], 1, 0))
        hid[sl, :] = h.astype(BF)
        pg[sl, :] = (d * dot(back[sl, :], down_ref[0], 1, 1)).astype(BF)
    ug = dot(xt[...], pg[...], 1, 0)
    dg = dot(hid[...], back[...], 0, 0)
    if acc:
        ug = ug + up_in[0]; dg = dg + down_in[0]
    ug_ref[0] = ug
    dg_ref[0] = dg
    if own:
        p = dot(hid[...], down_ref[0], 1, 0)
        r = dot(pg[...], up_ref[0], 1, 1)
        @pl.when(f == 0)
        def _():
            prod[...] = p
            rowg[...] = r
        @pl.when(f > 0)
        def _():
            prod[...] += p
            rowg[...] += r
        @pl.when(f == nf - 1)
        def _():
            gates = gates_s[...]
            gate = jnp.sum(jnp.where(mine, gates, 0.0), axis=1, keepdims=True)
            back[...] = (gate * prod[...]).astype(BF)
            per = R // groups
            for j in range(groups):
                got = back[pl.ds(pl.multiple_of((j ^ place_ref[0]) * per, per), per), :]
                w_refs[j // 4][j % 4] = got.reshape(w_refs[0].shape[1:])
            gg = jnp.sum(cots[...].astype(F32) * prod[...], axis=1, keepdims=True)
            lg = (gates * (jnp.where(mine, gg, 0.0) - gate * gg)).astype(BF)
            rg_ref[...] = (rowg[...] + dot(lg, rt_ref[...], 1, 1)).astype(BF).reshape(rg_ref.shape)
            og = dot(xt[...], lg, 1, 0)
            @pl.when(e == 0)
            def _():
                og_ref[...] = og
            @pl.when(e > 0)
            def _():
                og_ref[...] += og

def expert_call(own, place, xs, gs, full, up, down, experts, acc=None, first=0, span=None, tile=TILE):
    groups, imgs, lc, width = xs[0].shape
    local, _, ff = up.shape
    cap = lc // local
    planes = groups // 4
    R = groups * imgs * cap * len(xs)
    span = local if span is None else span
    block = pl.BlockSpec((groups, imgs, cap, width), lambda e, f: (0, 0, e + first, 0))
    upb = pl.BlockSpec((1, width, tile), lambda e, f: (e + first, 0, f))
    dnb = pl.BlockSpec((1, tile, width), lambda e, f: (e + first, f, 0))
    last = full.shape[1] // 128 - 1
    in_specs = [pl.BlockSpec(memory_space=pltpu.SMEM), pl.BlockSpec((width, 128), lambda e, f: (0, last)), upb, dnb]
    in_specs += [block] * len(xs)
    if own:
        in_specs += [pl.BlockSpec((1, imgs, cap, width), lambda e, f: (0, 0, e, 0))] * planes
        in_specs += [pl.BlockSpec((planes, 1, imgs, cap, width), lambda e, f: (0, 0, 0, e, 0)),
                     pl.BlockSpec((2 * planes, imgs, cap, width), lambda e, f: (0, 0, e, 0))]
    else:
        in_specs += [block] * len(gs)
    args = [place, full, up, down, *xs, *gs]
    out_shape, out_specs, alias = [], [], {}
    if own:
        out_shape += [jax.ShapeDtypeStruct((4, imgs, lc, width), BF)] * planes
        out_shape += [jax.ShapeDtypeStruct(xs[0].shape, BF)] * 2
        out_specs += [pl.BlockSpec((4, imgs, cap, width), lambda e, f: (0, 0, e, 0))] * planes + [block] * 2
    if acc is not None:
        at = len(args)
        alias = {at: len(out_shape), at + 1: len(out_shape) + 1}
        in_specs += [upb, dnb]
        args += list(acc)
    out_shape += [jax.ShapeDtypeStruct(up.shape, F32), jax.ShapeDtypeStruct(down.shape, F32)]
    out_specs += [upb, dnb]
    scratch = [pltpu.VMEM((width, R), BF), pltpu.VMEM((R, width), BF), pltpu.VMEM((R, width), BF)]
    if own:
        out_shape.append(jax.ShapeDtypeStruct((width, 128), F32))
        out_specs.append(pl.BlockSpec((width, 128), lambda e, f: (0, 0)))
        scratch.append(pltpu.VMEM((R, 128), F32))
    else:
        scratch.append(pltpu.VMEM((R, width), BF))
    scratch += [pltpu.VMEM((R, tile), BF), pltpu.VMEM((R, tile), BF)]
    if own:
        scratch += [pltpu.VMEM((R, width), F32)] * 2
    return pl.pallas_call(
        functools.partial(expert_kernel, own, acc is not None, experts, first, local, planes),
        grid=(span, ff // tile), in_specs=in_specs, out_specs=out_specs, out_shape=out_shape,
        scratch_shapes=scratch, input_output_aliases=alias,
        cost_estimate=pl.CostEstimate(flops=int((20 * 1.5 if own else 15 * 0.7 * span) * 1.15e9), bytes_accessed=1, transcendentals=0),
        compiler_params=pltpu.CompilerParams(vmem_limit_bytes=56 * 2**20, dimension_semantics=("arbitrary", "arbitrary")),
    )(*args)


def vec_rows(pack_ref, at):
    return pack_ref[:, at:].astype(F32).T


def slot_table(slot_ref, i, slots, at=0):
    rows = lax.broadcasted_iota(jnp.int32, (slots, slot_ref.shape[2]), 0)
    return ((rows == slot_ref[i, at : at + 1, :]) | (rows == slot_ref[i, at + 1 : at + 2, :])).astype(F32).astype(BF)


def route_kernel(experts, place_ref, meta_ref, cap_ref, cot_ref, slot_ref, *rest):
    rows_refs, wide = rest[:-1], rest[-1]
    groups = 4 * len(rows_refs) // CHUNKS
    per = experts * CAP // groups
    images, _, length = meta_ref.shape
    limit_of = cap_ref[...]
    first = cot_ref.shape[2] // 8 * 8
    wide[:, first:, :] = jnp.zeros((wide.shape[0], wide.shape[1] - first, wide.shape[2]), F32)
    real = cot_ref.shape[2]
    for i in range(images):
        meta = meta_ref[i]
        order = meta[2:3, :]
        earlier = (meta.T[:, 2:3] < order).astype(F32).astype(BF)
        labels = lax.broadcasted_iota(jnp.int32, (experts, length), 0).astype(F32)
        hits = [labels == meta[c : c + 1, :] for c in range(2)]
        ones = [h.astype(F32) for h in hits]
        before = [dot(ones[0].astype(BF), earlier, 1, 0)]
        before.append(dot(ones[1].astype(BF), earlier, 1, 0) + jnp.sum(ones[0], axis=1, keepdims=True))
        for c in range(2):
            position = jnp.sum(ones[c] * before[c], axis=0, keepdims=True)
            limit = jnp.sum(ones[c] * limit_of, axis=0, keepdims=True)
            slot = jnp.where(position < limit, meta[c : c + 1, :] * CAP + position, -1.0)
            slot = slot.astype(jnp.int32)
            slot_ref[i, c : c + 1, :] = slot
            near = slot ^ (place_ref[0] * per)
            slot_ref[i, 2 + c : 3 + c, :] = jnp.where(slot >= 0, near, -1)
        slot_ref[i, 4:, :] = jnp.full((4, length), -1, jnp.int32)
        wide[i, 0:real, :] = cot_ref[i, 0].astype(F32)
        rows = dot(slot_table(slot_ref, i, experts * CAP, 2), wide[i].astype(BF), 1, 0).astype(BF)
        planes = groups // 4
        count = rows_refs[0].shape[1]
        rows = rows.reshape(planes, 4, per, rows.shape[1])
        for k in range(planes):
            rows_refs[i // count * planes + k][:, i % count] = rows[k]


def route_call(place, meta, limits, cot, size):
    images, _, length = meta.shape
    experts = limits.shape[0]
    width = cot.shape[-1]
    vmem = pl.BlockSpec(memory_space=pltpu.VMEM)
    planes = size // 4
    return pl.pallas_call(
        functools.partial(route_kernel, experts),
        in_specs=[pl.BlockSpec(memory_space=pltpu.SMEM), vmem, vmem, vmem],
        out_shape=[jax.ShapeDtypeStruct((images, 8, length), jnp.int32)]
        + [jax.ShapeDtypeStruct((4, images // CHUNKS, experts * CAP // size, width), BF)] * (planes * CHUNKS),
        scratch_shapes=[pltpu.VMEM((images, length, width), F32)],
        cost_estimate=pl.CostEstimate(flops=3450000000, bytes_accessed=1, transcendentals=0),
        compiler_params=pltpu.CompilerParams(vmem_limit_bytes=48 * 2**20),
    )(place, meta, limits, cot)


def pack_kernel(attend_ref, output_ref, router_ref, vec_ref, out_ref, tall):
    rows, wide = attend_ref.shape
    width = output_ref.shape[1]
    out_ref[:, :wide] = attend_ref[...]
    out_ref[:, wide : wide + width] = output_ref[...]
    tall[...] = jnp.zeros_like(tall)
    experts = router_ref.shape[1]
    tall[0:rows, 0:experts] = router_ref[...].astype(F32)
    vecs = jnp.concatenate([vec_ref[...].astype(F32), jnp.zeros((4, 128), F32)], axis=0)
    turned = jnp.concatenate([vecs] + [jnp.zeros((120, 128), F32)], axis=0).T
    lane = lax.broadcasted_iota(jnp.int32, (128, 128), 1)
    full = jnp.where(lane < experts, tall[...], jnp.roll(turned, experts, axis=1))
    out_ref[:, wide + width :] = full[0:rows].astype(BF)


def half_masks(width):
    lane = lax.broadcasted_iota(jnp.int32, (1, width), 1)
    return [(lane < HEAD_DIM).astype(F32).astype(BF), (lane >= HEAD_DIM).astype(F32).astype(BF)]


def forward_kernel(tok_ref, pack_ref, slot_ref, rows_ref, normed_ref, joined_ref, probs_ref, mixed_ref,
                   middle_ref, wide, heads):
    images, _, real, width = tok_ref.shape
    length = slot_ref.shape[2]
    groups, _, per, _ = rows_ref.shape
    experts = groups * per // CAP
    vecs = vec_rows(pack_ref, 4 * width)[experts : experts + 4]
    gain_one, shift_one, gain_two, shift_two = (vecs[k : k + 1] for k in range(4))
    masks = half_masks(2 * HEAD_DIM)
    key_real = lax.broadcasted_iota(jnp.int32, (1, length), 1) < real
    first = real // 8 * 8
    wide[:, first:, :] = jnp.zeros((wide.shape[0], wide.shape[1] - first, wide.shape[2]), F32)
    for i in range(images):
        wide[i, 0:real, :] = tok_ref[i, 0].astype(F32)
        tokens = wide[i]
        hat, _ = norm_parts(tokens)
        normed = (hat * gain_one + shift_one).astype(BF)
        normed_ref[i] = normed
        joined = dot(normed, pack_ref[:, : 3 * width], 1, 0).astype(BF)
        joined_ref[i] = joined
        for pair in range(HEADS // 2):
            at = pair * 2 * HEAD_DIM
            q = joined[:, at : at + 2 * HEAD_DIM] * jnp.asarray(HEAD_DIM ** (-0.5), BF)
            k = joined[:, width + at : width + at + 2 * HEAD_DIM]
            v = joined[:, 2 * width + at : 2 * width + at + 2 * HEAD_DIM]
            both = None
            for s in range(2):
                scores = dot(q * masks[s], k, 1, 1)
                scores = jnp.where(key_real, scores, -1e30)
                raised = jnp.exp(scores - jnp.max(scores, axis=1, keepdims=True))
                probs = raised / jnp.sum(raised, axis=1, keepdims=True)
                probs = probs.astype(BF)
                probs_ref[i, 2 * pair + s] = probs
                got = dot(probs, v * masks[s], 1, 0)
                both = got if both is None else both + got
            heads[i, :, at : at + 2 * HEAD_DIM] = both.astype(BF)
        mixed = heads[i]
        mixed_ref[i] = mixed
        middle = tokens + dot(mixed, pack_ref[:, 3 * width : 4 * width], 1, 0)
        middle_ref[i] = middle
        hat_two, _ = norm_parts(middle)
        second = (hat_two * gain_two + shift_two).astype(BF)
        rows = dot(slot_table(slot_ref, i, groups * per), second, 1, 0)
        rows_ref[:, i] = rows.astype(BF).reshape(groups, per, width)


def whole(shape):
    return pl.BlockSpec(shape, lambda _: (0,) * len(shape))


def part_of(shape, count, chunk):
    return pl.BlockSpec((count,) + tuple(shape[1:]), lambda _: (chunk,) + (0,) * (len(shape) - 1))


def forward_call(chunk, count, tokens_in, pack, slot, size, slots):
    width = tokens_in.shape[-1]
    length = slot.shape[2]
    shapes = [((size, count, slots // size, width), BF), ((count, length, width), BF), ((count, length, 3 * width), BF),
              ((count, HEADS, length, length), BF), ((count, length, width), BF), ((count, length, width), F32)]
    return pl.pallas_call(
        forward_kernel, grid=(1,),
        in_specs=[part_of(tokens_in.shape, count, chunk), whole(pack.shape),
                  part_of(slot.shape, count, chunk)],
        out_specs=[whole(s) for s, _ in shapes],
        out_shape=[jax.ShapeDtypeStruct(s, d) for s, d in shapes],
        scratch_shapes=[pltpu.VMEM((count, length, width), F32), pltpu.VMEM((count, length, width), BF)],
        cost_estimate=pl.CostEstimate(flops=6440000000, bytes_accessed=1, transcendentals=0),
        compiler_params=pltpu.CompilerParams(vmem_limit_bytes=56 * 2**20),
    )(tokens_in, pack, slot)


def backward_kernel(chunk, acc, last, *refs):
    refs = list(refs)
    (rows_ref, slot_ref, tok_ref, cot_ref, pack_ref, normed_ref, joined_ref, probs_ref, mixed_ref,
     middle_ref) = refs[:10]
    refs = refs[10:]
    if acc:
        attend_in, output_in, vec_in = refs[:3]
        refs = refs[4:]
    if last:
        place_ref, router_in = refs[0], refs[1 : 1 + CHUNKS]
        refs = refs[1 + CHUNKS :]
        grad_ref, keep_ref, send_ref, wide, joined_grad, tall = refs
    else:
        grad_ref, attend_ref, output_ref, vec_ref, wide, joined_grad, tall = refs
    images, _, real, width = tok_ref.shape
    length = slot_ref.shape[2]
    groups, _, per, _ = rows_ref.shape
    experts = groups * per // CAP
    vecs = vec_rows(pack_ref, 4 * width)[experts : experts + 4]
    gain_one, _, gain_two, _ = (vecs[k : k + 1] for k in range(4))
    masks = half_masks(2 * HEAD_DIM)
    scale = HEAD_DIM ** (-0.5)
    attend_sum = output_sum = None
    sums = [None] * 4
    def add(old, new):
        return new if old is None else old + new
    first = real // 8 * 8
    wide[:, :, first:, :] = jnp.zeros(wide.shape[:2] + (wide.shape[2] - first, wide.shape[3]), F32)
    for i in range(images):
        wide[0, i, 0:real, :] = tok_ref[i, 0].astype(F32)
        wide[1, i, 0:real, :] = cot_ref[i, 0].astype(F32)
        table = slot_table(slot_ref, i, groups * per)
        second_grad = dot(table, rows_ref[:, i].reshape(groups * per, width), 0, 0)
        middle = middle_ref[i]
        hat_two, inv_two = norm_parts(middle)
        sums[2] = add(sums[2], jnp.sum(second_grad * hat_two, axis=0, keepdims=True))
        sums[3] = add(sums[3], jnp.sum(second_grad, axis=0, keepdims=True))
        middle_grad = wide[1, i] + norm_back(second_grad, hat_two, inv_two, gain_two)
        branch_grad = middle_grad.astype(BF)
        output_sum = add(output_sum, dot(mixed_ref[i], branch_grad, 0, 0))
        mixed_grad = dot(branch_grad, pack_ref[:, 3 * width : 4 * width], 1, 1).astype(BF)
        joined = joined_ref[i]
        for pair in range(HEADS // 2):
            at = pair * 2 * HEAD_DIM
            q = joined[:, at : at + 2 * HEAD_DIM]
            k = joined[:, width + at : width + at + 2 * HEAD_DIM]
            v = joined[:, 2 * width + at : 2 * width + at + 2 * HEAD_DIM]
            m = mixed_grad[:, at : at + 2 * HEAD_DIM]
            vg = qg = kg = None
            for s in range(2):
                low = probs_ref[i, 2 * pair + s]
                ms = m * masks[s]
                vg = add(vg, dot(low, ms, 0, 0))
                probs = low.astype(F32)
                probs_grad = dot(ms, v, 1, 1)
                weighed = probs * probs_grad
                scores_grad = (weighed - probs * jnp.sum(weighed, axis=1, keepdims=True)).astype(BF)
                qg = add(qg, dot(scores_grad, k * masks[s], 1, 0))
                kg = add(kg, dot(scores_grad, q * masks[s], 0, 0))
            joined_grad[i, :, at : at + 2 * HEAD_DIM] = (qg * scale).astype(BF)
            joined_grad[i, :, width + at : width + at + 2 * HEAD_DIM] = (kg * scale).astype(BF)
            joined_grad[i, :, 2 * width + at : 2 * width + at + 2 * HEAD_DIM] = vg.astype(BF)
        grads = joined_grad[i]
        attend_sum = add(attend_sum, dot(normed_ref[i], grads, 0, 0))
        normed_grad = dot(grads, pack_ref[:, : 3 * width], 1, 1)
        hat_one, inv_one = norm_parts(wide[0, i])
        sums[0] = add(sums[0], jnp.sum(normed_grad * hat_one, axis=0, keepdims=True))
        sums[1] = add(sums[1], jnp.sum(normed_grad, axis=0, keepdims=True))
        total = (middle_grad + norm_back(normed_grad, hat_one, inv_one, gain_one)).astype(BF)
        grad_ref[i, 0] = total[0:real]
    tall[...] = jnp.zeros_like(tall)
    for k in range(4):
        tall[experts + k : experts + k + 1, :] = sums[k]
    if acc:
        attend_sum = attend_sum + attend_in[...]
        output_sum = output_sum + output_in[...]
    vec = tall[...].T
    if acc:
        vec = vec + vec_in[...]
    if not last:
        attend_ref[...] = attend_sum
        output_ref[...] = output_sum
        vec_ref[...] = vec
        return
    odd = place_ref[0] % 2 == 1
    for part in router_in:
        vec = vec + part[...]
    for value, start in ((attend_sum, 0), (output_sum, 3 * width), (vec, 4 * width)):
        halves = value.reshape(groups // 2, 2, width // groups, value.shape[1])
        zero, one = (halves[:, k].reshape(width // 2, value.shape[1]) for k in range(2))
        at = slice(start, start + value.shape[1])
        keep_ref[:, at] = jnp.where(odd, one, zero)
        send_ref[:, at] = jnp.where(odd, zero, one).astype(BF)


def backward_call(chunk, count, rows, slot, tokens_in, cot, pack, saved, acc, final):
    width = tokens_in.shape[-1]
    length = slot.shape[2]
    args = [rows, slot, tokens_in, cot, pack] + list(saved)
    specs = [whole(rows.shape), part_of(slot.shape, count, chunk), part_of(tokens_in.shape, count, chunk),
             part_of(cot.shape, count, chunk), whole(pack.shape)] + [whole(s.shape) for s in saved]
    sums = [(width, 3 * width), (width, width), (width, 128)]
    alias = {}
    if acc is not None:
        args += list(acc[1:]) + [acc[0]]
        specs += [whole(s) for s in sums] + [pl.BlockSpec(memory_space=pl.ANY)]
        alias = {len(args) - 1: 0}
    kinds = [(s, F32) for s in sums]
    if final is not None:
        args += list(final)
        specs += [pl.BlockSpec(memory_space=pltpu.SMEM)] + [whole(v.shape) for v in final[1:]]
        kinds = [((width // 2, 4 * width + 128), d) for d in (F32, BF)]
    return pl.pallas_call(
        functools.partial(backward_kernel, chunk, acc is not None, final is not None), grid=(1,),
        in_specs=specs, out_specs=[part_of(tokens_in.shape, count, chunk)] + [whole(s) for s, _ in kinds],
        out_shape=[jax.ShapeDtypeStruct(tokens_in.shape, BF)] + [jax.ShapeDtypeStruct(s, d) for s, d in kinds],
        scratch_shapes=[pltpu.VMEM((2, count, length, width), F32), pltpu.VMEM((count, length, 3 * width), BF),
                        pltpu.VMEM((128, width), F32)],
        input_output_aliases=alias,
        cost_estimate=pl.CostEstimate(flops=8855000000, bytes_accessed=1, transcendentals=0),
        compiler_params=pltpu.CompilerParams(vmem_limit_bytes=56 * 2**20),
    )(*args)


def result_kernel(planes, slot_ref, side, core, *refs):
    far, middle, out_ref = refs[: planes * CHUNKS], refs[planes * CHUNKS : -1], refs[-1]
    images, real = out_ref.shape[0], out_ref.shape[2]
    count = middle[0].shape[0]
    for i in range(images):
        c, at = i // count, i % count
        rows = []
        for n in range(c * planes, (c + 1) * planes):
            rows += [far[n][0, at], core[n, at], side[n, 0, at], core[planes * CHUNKS + n, at]]
        rows = jnp.concatenate(rows, axis=0)
        table = slot_table(slot_ref, i, rows.shape[0], 2)
        out_ref[i, 0] = (middle[c][at] + dot(table, rows, 0, 0)).astype(BF)[0:real]


def result_call(far, side, core, slot, middle, shape):
    return pl.pallas_call(
        functools.partial(result_kernel, len(far) // CHUNKS), out_shape=jax.ShapeDtypeStruct(shape, BF),
        cost_estimate=pl.CostEstimate(flops=3450000000, bytes_accessed=1, transcendentals=0),
        compiler_params=pltpu.CompilerParams(vmem_limit_bytes=32 * 2**20),
    )(slot, side, core, *far, *middle)


def flips(size, bit):
    return [(i, i ^ bit) for i in range(size)]


def in_order(parts, index):
    while len(parts) > 1:
        half = len(parts) // 2
        high = (index // half) % 2 == 1
        low, top = parts[:half], parts[half:]
        parts_low = [jnp.where(high, t, l) for l, t in zip(low, top)]
        parts_top = [jnp.where(high, l, t) for l, t in zip(low, top)]
        index = index % half
        if half == 1:
            return [parts_low[0], parts_top[0]]
        return in_order(parts_low, index) + in_order(parts_top, index)
    return parts


def hop(v, size, bit):
    return lax.ppermute(v, "fsdp", flips(size, bit))


def gather_far(piece, size):
    far = [piece] + [hop(piece, size, 4 * k) for k in range(1, size // 4)]
    return jnp.stack(in_order(far, lax.axis_index("fsdp") // 4))


def gather_near(held, size, bit):
    came = hop(held, size, bit)
    axis = 1 if bit == 2 else 2
    mine = (lax.axis_index("fsdp") // bit) % 2
    side = lax.broadcasted_iota(jnp.int32, held.shape[:axis] + (2,) + held.shape[axis:], axis)
    return jnp.where(side == mine, jnp.expand_dims(held, axis), jnp.expand_dims(came, axis))


def side_hop(far, size):
    return hop(jnp.stack([p[2:4] for p in far]), size, 2)


def core_hop(far, side, size):
    return hop(jnp.concatenate([p[1:2] for p in far] + [side[:, 1]]), size, 1)


def after(value, *others):
    return lax.optimization_barrier((value,) + others)[0]


def scatter_sum(keep, send, size, replicas, between, *wait):
    index = lax.axis_index("fsdp")
    planes = size // 4
    held = keep + hop(send, size, 1).astype(F32)
    rows = held.shape[0] // (planes * 2)
    held = held.reshape(planes, 2, rows, -1)
    high = (index // 2) % 2 == 1
    gone = jnp.where(high, held[:, 0], held[:, 1]).astype(BF)
    between[0](gone)
    came = hop(after(gone, *wait), size, 2)
    held = jnp.where(high, held[:, 1], held[:, 0]) + came.astype(F32)
    low = held.astype(BF)
    place = index // 4
    total = lax.dynamic_index_in_dim(held, place, 0, keepdims=False)
    gone = [lax.dynamic_index_in_dim(low, place ^ k, 0, keepdims=False) for k in range(1, planes)]
    between[1](gone[0])
    for k in range(1, planes):
        total = total + hop(gone[k - 1], size, 4 * k).astype(F32)
    if replicas == 2:
        low = total.astype(BF)
        between[2](low)
        return low.astype(F32) + lax.ppermute(low, "replica", [(0, 1), (1, 0)]).astype(F32)
    return lax.psum(total, "replica")


def solution(mesh):
    replicas = mesh.shape["replica"]
    size = mesh.shape["fsdp"]

    def body(tokens_in, picks_in, ranks_in, capacity, first_gain, first_shift, attend_weight,
             output_weight, second_gain, second_shift, router_weight, expert_up, expert_down, cotangent):
        micro, _, length, width = tokens_in.shape
        experts = capacity.shape[0]
        slots = experts * CAP
        tall = -(-length // 128) * 128
        share = attend_weight.shape[0]
        vecs = jnp.stack([first_gain, first_shift, second_gain, second_shift])
        vecs = jnp.pad(vecs, ((0, 0), (0, 128 - share)))
        packed = pl.pallas_call(
            pack_kernel, out_shape=jax.ShapeDtypeStruct((share, 4 * width + 128), BF),
            cost_estimate=pl.CostEstimate(flops=2300000000, bytes_accessed=1, transcendentals=0),
        scratch_shapes=[pltpu.VMEM((128, 128), F32)],
        )(attend_weight, output_weight, router_weight, vecs)
        far = gather_far(packed, size)

        place = lax.axis_index("fsdp").astype(jnp.int32).reshape(1)
        meta = jnp.concatenate([picks_in[:, 0].transpose(0, 2, 1), ranks_in], axis=1).astype(F32)
        meta = jnp.pad(meta, ((0, 0), (0, 5), (0, tall - length)), constant_values=1000.0)
        slot, *cot_out = route_call(place, meta, capacity.astype(F32)[:, None], cotangent, size)
        count = micro // CHUNKS
        chunks = range(CHUNKS)
        near = gather_near(after(far, slot), size, 2)
        planes = size // 4

        def along_z(pieces, *wait):
            ready = lax.optimization_barrier((*wait, *pieces))[len(wait) :]
            return [q if k == 0 else hop(q, size, 4 * k) for k, q in enumerate(ready)]

        cot_far = [along_z(cot_out[c * planes : (c + 1) * planes], near if c else far) for c in chunks[:1 if F7 else None]]
        full = gather_near(near, size, 1).reshape(size * share, -1)

        def exchange(r):
            return lax.all_to_all(r, "fsdp", split_axis=0, concat_axis=0, tiled=True)

        def swap(v):
            return lax.ppermute(v, "replica", [(0, 1), (1, 0)])

        rows_in, cot_rows, saved = [], [], []
        for c in chunks:
            sent, *kept = forward_call(c, count, tokens_in, full, slot, size, slots)
            saved.append(kept)
            rows_in.append(exchange(after(sent, *cot_far[c])))
            arrived = lax.optimization_barrier((sent, *cot_far[c]))[1:]
            side = side_hop(arrived, size)
            cot_rows.append((*arrived, side, core_hop(arrived, side, size)))
            if F7 and c + 1 < CHUNKS:
                cot_far.append(along_z(cot_out[(c + 1) * planes : (c + 2) * planes], *((sent,) if F7 == 1 else (cot_far[0][1 : 1 + F7]))))
        paired = replicas == 2
        other_x = [swap(x) for x in rows_in] if paired else [()] * CHUNKS

        acc = None
        row_grads, router_grads, cot_kept, result_far = [], [], [], []
        for c in chunks:
            ready = after(place, other_x[c - 1]) if c > 0 and F1 else place
            *w, r, kept, ug, dg, og = expert_call(True, ready, rows_in[c : c + 1], cot_rows[c], full,
                                                  expert_up, expert_down, experts, acc)
            acc = (ug, dg)
            row_grads.append(exchange(r))
            router_grads.append(og)
            cot_kept.append(kept)
            result_far.append(along_z(w))
        other_g = [swap(g) for g in cot_kept] if paired else [()] * CHUNKS
        box = [acc]

        def other(first, span, *wait):
            if paired:
                box[0] = expert_call(False, after(place, *wait), other_x, other_g, full,
                                     expert_up, expert_down, experts, box[0], first, span)

        sums = None
        half = expert_up.shape[0] // 2
        for c in chunks:
            last = c == CHUNKS - 1
            final = (after(place, box[0][0]) if F9 else place, *router_grads) if last else None
            slots_in = slot
            if c == 0 and F2 > 0:
                slots_in = after(slot, other_g[0], *other_x[: F2])
            if c == 1 and F3 > 0:
                slots_in = after(slot, *other_g, *other_x)
            if (F4, F5)[c] > 0:
                slots_in = after(slots_in, *result_far[c][1 : 1 + (F4, F5)[c]])
            sums = backward_call(c, count, row_grads[c], slots_in, tokens_in, cotangent, full, saved[c], sums, final)
            if c == CHUNKS - 2:
                other(0, half, sums[1])
                early = box[0][0]
                if F8 == 5:
                    other(half, half)
        token_grad, keep, send = sums
        every = [p for far in result_far for p in far]
        if F7 != 9:
            every = list(lax.optimization_barrier((early if G else keep, *every))[1:])
        side = side_hop(every, size)
        tail = []
        total = scatter_sum(keep, send, size, replicas,
                            (lambda gone: other(half, half, gone) if F8 == 0 else None,
                             lambda gone: (tail.append(gone), other(half, half, gone) if F8 == 2 else None), tail.append),
                            *((side,) if F10 else ()))
        acc = box[0]
        if not paired:
            acc = lax.psum(tuple(acc), "replica")
        up_grad, down_grad = acc
        side_in = side
        if F6:
            late = (tail[F6 - 1],) if F6 < 3 else (box[0][0],) if F6 == 4 else (box[0][0], tail[0])
            side_in = after(side, *late)
        out = result_call(every, side, core_hop(every, side_in, size), after(slot, *tail), [s[4] for s in saved], tokens_in.shape)

        w = 4 * width + experts
        return (out, token_grad, total[:, w], total[:, w + 1], total[:, : 3 * width], total[:, 3 * width : 4 * width],
                total[:, w + 2], total[:, w + 3], total[:, 4 * width : w], up_grad, down_grad)

    split = ("replica", "fsdp")
    in_specs = (P(None, split), P(None, split), P(None, split), P(), P("fsdp"), P("fsdp"), P("fsdp"), P("fsdp"),
                P("fsdp"), P("fsdp"), P("fsdp"), P("fsdp"), P("fsdp"), P(None, split))
    out_specs = (P(None, split), P(None, split)) + (P("fsdp"),) * 9
    return jax.shard_map(body, mesh=mesh, in_specs=in_specs, out_specs=out_specs, check_vma=False)
```
